128 devices in a mesh: tmpl: 4 (over z_hi, core), row: 32 (over y, z_lo, x).
Axes of the slice: x: 4, y: 4, z: 4 (z_hi: 2, z_lo: 2; z = z_hi * 2 + z_lo), core: 2. Of those that a mesh axis runs over, the one named last changes fastest.
Arguments:
- template_pair: bfloat16 [4, 256, 256, 64], P('tmpl', 'row'), may hold values from -6 to 6
- template_mask: int32 [4, 256], replicated, may hold values 0 or 1
- residue_index: int32 [256], replicated, may hold values from 0 to 509, as said below
- query_pair: bfloat16 [256, 256, 128], P('row'), may hold values from -6 to 6
- relpos_table: bfloat16 [128, 64], replicated, may hold values from -3 to 3
- norm_gain: float32 [64], replicated, may hold values from 0.5 to 1.5
- left_weight: bfloat16 [64, 64], replicated, may hold values from -0.75 to 0.75
- right_weight: bfloat16 [64, 64], replicated, may hold values from -0.75 to 0.75
- gate_weight: bfloat16 [64, 64], replicated, may hold values from -0.75 to 0.75
- out_weight: bfloat16 [64, 64], replicated, may hold values from -0.75 to 0.75
- tri_gain: float32 [64], replicated, may hold values from 0.5 to 1.5
- pair_gain: float32 [64], replicated, may hold values from 0.5 to 1.5
- kv_weight: bfloat16 [64, 128], replicated, may hold values from -0.75 to 0.75
- query_gain: float32 [128], replicated, may hold values from 0.5 to 1.5
- query_weight: bfloat16 [128, 64], replicated, may hold values from -0.5 to 0.5
- attn_out_weight: bfloat16 [64, 128], replicated, may hold values from -0.75 to 0.75
- cotangent: bfloat16 [256, 256, 128], P('row'), may hold values from -6 to 6
Outputs:
- template_grad: float32 [4, 256, 256, 64], P('tmpl', 'row')
- query_grad: float32 [256, 256, 128], P('row')
- projection_grad: float32 [2, 64, 64], replicated
The draws below stay inside these ranges and needn't reach their ends.
Inputs may be any that keep to these rules, and one draw needn't show every extreme that they name: `residue_index`: strictly increasing, starting at 0, steps of 1 or 3, exactly (255) // 2 of them 3.
All inputs are finite; a program needn't handle non-finite values.
Results may differ from the reference program's by a relative error of at most 0.013.
Values may be sent and summed in bfloat16 or wider, within the bound.
No kernel may reach another device: no remote copies, remote signals or barrier semaphores. Data moves between devices by JAX's collectives and lax.ppermute only.
A program may use at most 128 MiB of HBM per device.

```python
import jax
import jax.numpy as jnp
from jax import lax

C = 64
Q = 128
HEADS = 4
HEAD_DIM = 16
BINS = 128
HD = 64
N_RES = 256
TEMPLATES = 4


def draw_residue_index(key, part):
    key = jax.random.fold_in(key, 5)
    count = N_RES - 1
    order = jax.random.permutation(key, jnp.arange(count, dtype=jnp.int32))
    steps_drawn = jnp.where(order < count // 2, 3, 1).astype(jnp.int32)
    start = jnp.zeros((1,), jnp.int32)
    return jnp.concatenate([start, jnp.cumsum(steps_drawn).astype(jnp.int32)]).astype(jnp.int32)


def with_ends(entries, key, smallest, top_value):
    longest = entries.shape.index(max(entries.shape))
    spots = []
    for shift in (0, 1):
        where = [jax.random.randint(jax.random.fold_in(key, axis), (), 0, length) for axis, length in enumerate(entries.shape)]
        where[longest] = (where[longest] + shift) % entries.shape[longest]
        spots.append(tuple(where))
    return entries.at[spots[0]].set(smallest).at[spots[1]].set(top_value)


def block_levels(rng, shape, shards, least, top_value):
    def one(dim, parts):
        heights = jax.random.uniform(jax.random.fold_in(jax.random.fold_in(rng, 6), dim), (parts,), jnp.float32, least / len(shards), top_value / len(shards))
        return jnp.repeat(jnp.exp(heights), shape[dim] // parts).reshape((-1,) + (1,) * (len(shape) - dim - 1))

    level = one(*shards[0])
    for cut in shards[1:]:
        level = level * one(*cut)
    return level


def centred(stream_key, extent, scale, most, cuts=(), kind=jnp.bfloat16):
    drawn = jax.random.normal(stream_key, extent, jnp.float32) * scale
    if len(cuts) > 0:
        drawn = block_levels(stream_key, extent, cuts, -0.22, 0.18) * drawn
    return jnp.clip(drawn, min=-most, max=most).astype(kind)


def setup_inputs(seed: int = 0) -> dict:
    key_list = jax.random.split(jax.random.key(seed), 18)
    template_pair = centred(key_list[0], (TEMPLATES, N_RES, N_RES, C), 1.0, 6.0, ((0, 4), (1, 32)))
    template_mask = with_ends((jax.random.randint(key_list[1], (TEMPLATES, N_RES), 0, 8) < 7).astype(jnp.int32), jax.random.fold_in(key_list[1], 1), 0, 1)
    residue_index = draw_residue_index(jax.random.fold_in(key_list[17], 71), 0)
    query_pair = centred(key_list[3], (N_RES, N_RES, Q), 1.0, 6.0, ((0, 32),))
    relpos_table = centred(key_list[4], (BINS, C), 0.5, 3.0)
    norm_gain = jnp.clip(1.0 + 0.1 * jax.random.normal(key_list[5], (C,), jnp.float32), 0.5, 1.5)
    left_weight = centred(key_list[6], (C, C), C ** -0.5, 0.75)
    right_weight = centred(key_list[7], (C, C), C ** -0.5, 0.75)
    gate_weight = centred(key_list[8], (C, C), C ** -0.5, 0.75)
    out_weight = centred(key_list[9], (C, C), C ** -0.5, 0.75)
    tri_gain = jnp.clip(1.0 + 0.1 * jax.random.normal(key_list[10], (C,), jnp.float32), 0.5, 1.5)
    pair_gain = jnp.clip(1.0 + 0.1 * jax.random.normal(key_list[11], (C,), jnp.float32), 0.5, 1.5)
    kv_weight = centred(key_list[12], (C, 2 * HD), C ** -0.5, 0.75)
    query_gain = jnp.clip(1.0 + 0.1 * jax.random.normal(key_list[13], (Q,), jnp.float32), 0.5, 1.5)
    query_weight = centred(key_list[14], (Q, HD), Q ** -0.5, 0.5)
    attn_out_weight = centred(key_list[15], (HD, Q), HD ** -0.5, 0.75)
    cotangent = centred(key_list[16], (N_RES, N_RES, Q), 1.0, 6.0, ((0, 32),))
    return {"template_pair": template_pair, "template_mask": template_mask, "residue_index": residue_index, "query_pair": query_pair, "relpos_table": relpos_table, "norm_gain": norm_gain, "left_weight": left_weight, "right_weight": right_weight, "gate_weight": gate_weight, "out_weight": out_weight, "tri_gain": tri_gain, "pair_gain": pair_gain, "kv_weight": kv_weight, "query_gain": query_gain, "query_weight": query_weight, "attn_out_weight": attn_out_weight, "cotangent": cotangent}


def layer_norm(x, gain):
    mean = lax.optimization_barrier(jnp.mean(x, -1, keepdims=True))
    cent = x - mean
    var = lax.optimization_barrier(jnp.mean(cent * cent, -1, keepdims=True))
    return cent * lax.rsqrt(var + 1e-05) * gain

def high_dot(a, b):
    return jnp.einsum('...c,cd->...d', a, b, precision=lax.Precision.HIGHEST)

def relative(res_rows, res_all, table):
    half = table.shape[0] // 2
    offset = jnp.clip(res_rows[:, None] - res_all[None, :], -half, half - 1) + half
    bins = jnp.arange(table.shape[0], dtype=jnp.int32)
    onehot = (offset[:, :, None] == bins[None, None, :]).astype(jnp.bfloat16)
    return jnp.dot(onehot, table, preferred_element_type=jnp.float32)

def project(ln_b, weight, mask_rows, mask_all):
    raw = jnp.dot(ln_b, weight, preferred_element_type=jnp.float32)
    return (raw * mask_rows[:, None, None] * mask_all[None, :, None]).astype(jnp.bfloat16)

def post_block(ln, z_in, tri, gate_w, out_w, tri_gain, pair_gain, kv_w):
    gate = jax.nn.sigmoid(high_dot(ln, gate_w))
    update = gate * high_dot(layer_norm(tri, tri_gain), out_w)
    return high_dot(layer_norm(z_in + update, pair_gain), kv_w)

def query_heads(query, gain, weight):
    return high_dot(layer_norm(query, gain), weight) * HEAD_DIM ** (-0.5)

def reference(template_pair, template_mask, residue_index, query_pair, relpos_table, norm_gain, left_weight, right_weight, gate_weight, out_weight, tri_gain, pair_gain, kv_weight, query_gain, query_weight, attn_out_weight, cotangent):
    f32 = jnp.float32
    rel = relative(residue_index, residue_index, relpos_table)
    gate_f, out_f, kv_f = (gate_weight.astype(f32), out_weight.astype(f32), kv_weight.astype(f32))
    saved = []
    for tindex in range(TEMPLATES):
        z_in = template_pair[tindex].astype(f32) + rel
        ln, ln_back = jax.vjp(lambda x: layer_norm(x, norm_gain), z_in)
        ln_b = ln.astype(jnp.bfloat16)
        mask = template_mask[tindex].astype(f32)
        left = project(ln_b, left_weight, mask, mask)
        right = project(ln_b, right_weight, mask, mask)
        tri = jnp.einsum('ikc,jkc->ijc', left.astype(f32), right.astype(f32), precision=lax.Precision.HIGHEST)
        kv, post_back = jax.vjp(lambda a, b, c: post_block(a, b, c, gate_f, out_f, tri_gain, pair_gain, kv_f), ln, z_in, tri)
        saved.append((ln_back, ln_b, mask, left, right, post_back, kv.astype(jnp.bfloat16)))
    query_f = query_pair.astype(f32)
    qh, query_back = jax.vjp(lambda x: query_heads(x, query_gain, query_weight.astype(f32)), query_f)
    qh4 = qh.reshape(N_RES, N_RES, HEADS, HEAD_DIM)
    keys, values, scores, pairs = ([], [], [], [])
    for tindex in range(TEMPLATES):
        kv_b = saved[tindex][6].astype(f32)
        key = kv_b[..., :HD].reshape(N_RES, N_RES, HEADS, HEAD_DIM)
        value = kv_b[..., HD:].reshape(N_RES, N_RES, HEADS, HEAD_DIM)
        mask = saved[tindex][2]
        pair = mask[:, None] * mask[None, :]
        bias = (pair - 1.0) * 1000000000.0
        scores.append(lax.optimization_barrier(jnp.sum(qh4 * key, -1)) * pair[:, :, None] + bias[:, :, None])
        keys.append(key)
        values.append(value)
        pairs.append(pair)
    scores = jnp.stack(scores)
    top = lax.optimization_barrier(jnp.max(scores, 0))
    expo = jnp.exp(scores - top[None])
    probs = expo / lax.optimization_barrier(jnp.sum(expo, 0))[None]
    attended = sum((probs[t][..., None] * values[t] for t in range(TEMPLATES)))
    d_o = jnp.dot(cotangent, attn_out_weight.T, preferred_element_type=f32).reshape(N_RES, N_RES, HEADS, HEAD_DIM)
    delta = lax.optimization_barrier(jnp.sum(d_o * attended, -1))
    d_qh = jnp.zeros_like(qh4)
    grads_t = []
    d_wl = jnp.zeros((C, C), f32)
    d_wr = jnp.zeros((C, C), f32)
    for tindex in range(TEMPLATES):
        ds = probs[tindex] * (lax.optimization_barrier(jnp.sum(d_o * values[tindex], -1)) - delta) * pairs[tindex][:, :, None]
        d_qh = d_qh + ds[..., None] * keys[tindex]
        d_key = (ds[..., None] * qh4).reshape(N_RES, N_RES, HD)
        d_value = (probs[tindex][..., None] * d_o).reshape(N_RES, N_RES, HD)
        d_kv = jnp.concatenate([d_key, d_value], -1)
        ln_back, ln_b, mask, left, right, post_back, kvb = saved[tindex]
        d_ln_a, d_zin_a, d_tri = post_back(d_kv)
        d_tri_b = d_tri.astype(jnp.bfloat16).astype(f32)
        mask2 = mask[:, None, None] * mask[None, :, None]
        d_left = (jnp.einsum('ijc,jkc->ikc', d_tri_b, right.astype(f32), precision=lax.Precision.HIGHEST) * mask2).astype(jnp.bfloat16)
        d_right = (jnp.einsum('ijc,ikc->jkc', d_tri_b, left.astype(f32), precision=lax.Precision.HIGHEST) * mask2).astype(jnp.bfloat16)
        d_ln_b = jnp.dot(d_left, left_weight.T, preferred_element_type=f32) + jnp.dot(d_right, right_weight.T, preferred_element_type=f32)
        d_wl = d_wl + jnp.einsum('ikc,ikd->cd', ln_b.astype(f32), d_left.astype(f32), precision=lax.Precision.HIGHEST)
        d_wr = d_wr + jnp.einsum('ikc,ikd->cd', ln_b.astype(f32), d_right.astype(f32), precision=lax.Precision.HIGHEST)
        grads_t.append(ln_back(d_ln_a + d_ln_b)[0] + d_zin_a)
    query_grad = query_back(d_qh.reshape(N_RES, N_RES, HD))[0]
    return (jnp.stack(grads_t), query_grad, jnp.stack([d_wl, d_wr]))
```

```python
import functools

import jax
import jax.numpy as jnp
from jax import lax
from jax.experimental import pallas as pl
from jax.experimental.pallas import tpu as pltpu
from jax.sharding import PartitionSpec as P

F32 = jnp.float32
BF16 = jnp.bfloat16
HEADS = 4
HEAD_DIM = 16
C = 64
ROWS = 8
N = 256
SHARDS = 32
VMEM = pl.BlockSpec(memory_space=pltpu.VMEM)
SMEM = pl.BlockSpec(memory_space=pltpu.SMEM)


def dot(a, b, contract=((1,), (0,))):
    return lax.dot_general(a, b, (contract, ((), ())), preferred_element_type=F32)


def flip(x):
    return x.astype(F32).T


def column(row, lanes=N):
    tall = jnp.broadcast_to(row, (128, row.shape[1])).T
    return jnp.concatenate([tall] * (lanes // 128), axis=1)


def hat(x):
    mean = jnp.mean(x, 0, keepdims=True)
    cent = x - mean
    var = jnp.mean(cent * cent, 0, keepdims=True)
    rstd = lax.rsqrt(var + 1e-05)
    return cent * rstd, rstd


def hat_back(dy, xhat, rstd):
    return rstd * (dy - jnp.mean(dy, 0, keepdims=True) - xhat * jnp.mean(dy * xhat, 0, keepdims=True))


def put_rows(spread, first, step, x):
    for half in range(2):
        spread[half, pl.ds(first, x.shape[0], stride=step), :] = x[:, 128 * half : 128 * half + 128]


def take_rows(wide, first, step):
    return jnp.concatenate([wide[half, pl.ds(first, SHARDS, stride=step), :] for half in range(2)], axis=1)


def pack(spread, out):
    for half in range(2):
        out[:, :, 128 * half : 128 * half + 128] = spread[half].reshape(out.shape[0], out.shape[1], 128).astype(BF16)


def unpack(x, wide):
    for half in range(2):
        wide[half] = x[:, :, 128 * half : 128 * half + 128].astype(F32).reshape(wide.shape[1], 128)


def place(rows_ref):
    t = lax.axis_index("tmpl")
    start = lax.axis_index("row") * ROWS
    mask_row = rows_ref[pl.ds(t, 1), :].astype(F32)
    return t, start, mask_row


def project_kernel(pair, mask, mask_s, res, res_s, table, gain, wl, wr, lr_out, z_out, spread):
    t, start, mask_row = place(mask)
    weight = jnp.concatenate([flip(wl[...]), flip(wr[...])], axis=0).astype(BF16)
    table_t = flip(table[...]).astype(BF16)
    g = column(gain[...])
    residues = res[...]
    bins = lax.broadcasted_iota(jnp.int32, (128, N), 0)

    def body(i, carry):
        offset = jnp.clip(res_s[start + i] - residues, -64, 63) + 64
        onehot = jnp.where(bins == offset, 1.0, 0.0).astype(BF16)
        z = flip(pair[i]) + dot(table_t, onehot)
        z_out[i] = z
        ln_b = (hat(z)[0] * g).astype(BF16)
        both = dot(weight, ln_b) * (mask_row * mask_s[t, start + i].astype(F32))
        for q in range(4):
            put_rows(spread, 8 * q + i, 32, both[32 * q : 32 * q + 32])
        return carry

    lax.fori_loop(0, ROWS, body, 0)
    pack(spread, lr_out)


def tri_kernel(lr, tri_out, mats_out):
    wide = lr[...].astype(F32)
    mats = [wide[:, 8 * q : 8 * q + 8, :].reshape(N, N).astype(BF16) for q in range(4)]
    for q in range(4):
        mats_out[q] = mats[q]
    parts = [dot(mats[cc], mats[2 + cc], ((1,), (1,))).reshape(SHARDS, 8, N) for cc in range(2)]
    tri_out[...] = jnp.concatenate(parts, axis=1).astype(BF16)


def heads_sum(x):
    return jnp.sum(x.reshape(HEADS, HEAD_DIM, N), axis=1)


def heads_spread(x):
    return jnp.broadcast_to(x[:, None, :], (HEADS, HEAD_DIM, N)).reshape(C, N)


def attend_kernel(
    tri, z, query, cot, mask, mask_s, norm_gain, wg, wo, tri_gain, pair_gain, wkv, q_gain, wq, wao,
    sg_out, that_out, yhat_out, gate_out, upd_out, qh_out, do_out, kv_out, rstd_out, wide,
):
    t, start, mask_row = place(mask)
    unpack(tri, wide)
    wg_t = flip(wg[...]).astype(BF16)
    wo_t = flip(wo[...]).astype(BF16)
    wkv_t = flip(wkv[...]).astype(BF16)
    wq_t = flip(wq[...]).astype(BF16)
    wao_v = wao[...]
    g_norm, g_tri, g_pair = column(norm_gain[...]), column(tri_gain[...]), column(pair_gain[...])
    g_query = q_gain[...]

    def body(i, carry):
        x = query[i].astype(F32)
        cent = x - jnp.mean(x, -1, keepdims=True)
        var = jnp.mean(cent * cent, -1, keepdims=True)
        qn = (cent * lax.rsqrt(var + 1e-05) * g_query).astype(BF16)
        qh = dot(wq_t, qn, ((1,), (1,))) * HEAD_DIM ** (-0.5)
        d_o = dot(wao_v, cot[i], ((1,), (1,)))
        qh_out[i] = qh
        do_out[i] = d_o

        tri_i = jnp.concatenate([take_rows(wide, i, 16), take_rows(wide, 8 + i, 16)], axis=0)
        that, rstd_t = hat(tri_i)
        upd = dot(wo_t, (that * g_tri).astype(BF16))
        z_i = z[i]
        gate = jax.nn.sigmoid(dot(wg_t, (hat(z_i)[0] * g_norm).astype(BF16)))
        yhat, rstd_y = hat(z_i + gate * upd)
        kv = dot(wkv_t, (yhat * g_pair).astype(BF16)).astype(BF16)
        kv_f = kv.astype(F32)
        pm = mask_row * mask_s[t, start + i].astype(F32)
        score = heads_sum(qh * kv_f[:C]) * pm + (pm - 1.0) * 1000000000.0
        dot_v = heads_sum(d_o * kv_f[C:])
        sg_out[i] = jnp.concatenate([score, dot_v], axis=0)
        that_out[i] = that
        yhat_out[i] = yhat
        gate_out[i] = gate
        upd_out[i] = upd
        kv_out[i] = kv
        rstd_out[i] = jnp.concatenate([jnp.broadcast_to(rstd_t, (4, N)), jnp.broadcast_to(rstd_y, (4, N))], axis=0)
        return carry

    lax.fori_loop(0, ROWS, body, 0)


def back_kernel(
    sg, that, yhat, gate, upd, qh, do, kv, rstd, mask, mask_s, wg, wo, tri_gain, pair_gain, wkv,
    dtri_out, dln_out, dzin_out, dqh_out, spread,
):
    t, start, mask_row = place(mask)
    g_tri, g_pair = column(tri_gain[...]), column(pair_gain[...])
    wg_v, wo_v, wkv_v = wg[...], wo[...], wkv[...]

    def body(i, carry):
        pm = mask_row * mask_s[t, start + i].astype(F32)
        every = [sg[s, i] for s in range(4)]
        own = sg[t, i]
        top = jnp.maximum(jnp.maximum(every[0][:4], every[1][:4]), jnp.maximum(every[2][:4], every[3][:4]))
        expo = [jnp.exp(e[:4] - top) for e in every]
        inv = 1.0 / (expo[0] + expo[1] + expo[2] + expo[3])
        delta = sum(ex * e[4:] for ex, e in zip(expo, every)) * inv
        prob = jnp.exp(own[:4] - top) * inv
        ds = heads_spread(pm * prob * (own[4:] - delta))
        p = heads_spread(prob)
        d_kv = jnp.concatenate([ds * qh[i], p * do[i]], axis=0).astype(BF16)
        dqh_out[i] = (ds * kv[i].astype(F32)[:C]).astype(BF16)
        rs = rstd[i]
        d_y = hat_back(dot(wkv_v, d_kv) * g_pair, yhat[i], rs[4:5])
        gate_i = gate[i]
        d_gpre = d_y * upd[i] * gate_i * (1.0 - gate_i)
        dln_out[i] = dot(wg_v, d_gpre.astype(BF16))
        dzin_out[i] = d_y
        d_tn = dot(wo_v, (d_y * gate_i).astype(BF16)) * g_tri
        d_tri = hat_back(d_tn, that[i], rs[0:1])
        put_rows(spread, i, 16, d_tri[:32])
        put_rows(spread, 8 + i, 16, d_tri[32:])
        return carry

    lax.fori_loop(0, ROWS, body, 0)
    pack(spread, dtri_out)


def tri_back_kernel(dtri, mats, out):
    wide = dtri[...].astype(F32)
    d = [wide[:, 8 * cc : 8 * cc + 8, :].reshape(N, N).astype(BF16) for cc in range(2)]
    parts = [dot(d[cc], mats[2 + cc]) for cc in range(2)]
    parts += [dot(d[cc], mats[cc], ((0,), (0,))) for cc in range(2)]
    out[...] = jnp.concatenate([p.reshape(SHARDS, 8, N) for p in parts], axis=1).astype(BF16)


def final_kernel(dlr, z, dln, dzin, mask, mask_s, norm_gain, wl, wr, grad_out, proj_out, wide):
    t, start, mask_row = place(mask)
    unpack(dlr, wide)
    g = column(norm_gain[...])
    weight = jnp.concatenate([wl[...], wr[...]], axis=1)

    def body(i, total):
        pm = mask_row * mask_s[t, start + i].astype(F32)
        parts = [take_rows(wide, 8 * q + i, 32) for q in range(4)]
        d = (jnp.concatenate(parts, axis=0) * pm).astype(BF16)
        zhat, rstd = hat(z[i])
        total = total + dot((zhat * g).astype(BF16), d, ((1,), (1,)))
        dy = (dln[i] + dot(weight, d)) * g
        grad_out[i] = (dzin[i] + hat_back(dy, zhat, rstd)).T
        return total

    proj_out[...] = lax.fori_loop(0, ROWS, body, jnp.zeros((C, 2 * C), F32))


def query_kernel(query, dqh, gain, wq, out):
    g = gain[...] * HEAD_DIM ** (-0.5)
    wq_v = wq[...]

    def body(i, carry):
        x = query[i].astype(F32)
        cent = x - jnp.mean(x, -1, keepdims=True)
        var = jnp.mean(cent * cent, -1, keepdims=True)
        rstd = lax.rsqrt(var + 1e-05)
        xhat = cent * rstd
        dy = dot(dqh[i].astype(BF16), wq_v, ((0,), (1,))) * g
        out[i] = rstd * (dy - jnp.mean(dy, -1, keepdims=True) - xhat * jnp.mean(dy * xhat, -1, keepdims=True))
        return carry

    lax.fori_loop(0, ROWS, body, 0)


def call(kernel, outs, specs, scratch=()):
    return pl.pallas_call(
        kernel,
        out_shape=[jax.ShapeDtypeStruct(s, d) for s, d in outs],
        in_specs=specs,
        out_specs=[VMEM] * len(outs),
        scratch_shapes=[pltpu.VMEM(s, F32) for s in scratch],
        compiler_params=pltpu.CompilerParams(vmem_limit_bytes=40 * 1024 * 1024),
    )


def swap(x, axis, size, bit):
    return lax.ppermute(x, axis, [(i, i ^ bit) for i in range(size)])


def local(
    template_pair, template_mask, residue_index, query_pair, relpos_table, norm_gain, left_weight, right_weight,
    gate_weight, out_weight, tri_gain, pair_gain, kv_weight, query_gain, query_weight, attn_out_weight, cotangent,
):
    pair = template_pair[0]
    row = lambda x: x.reshape(1, -1)
    every = functools.partial(lax.all_to_all, axis_name="row", split_axis=0, concat_axis=0, tiled=True)
    lr, z = call(
        project_kernel,
        [((SHARDS, 32, N), BF16), ((ROWS, C, N), F32)],
        [VMEM, VMEM, SMEM, VMEM, SMEM] + [VMEM] * 4,
        [(2, SHARDS * 32, 128)],
    )(
        pair, template_mask, template_mask, row(residue_index), residue_index, relpos_table, row(norm_gain),
        left_weight, right_weight,
    )
    lr = every(lr)
    tri, mats = call(tri_kernel, [((SHARDS, 16, N), BF16), ((4, N, N), BF16)], [VMEM])(lr)
    tri = every(tri)
    sg, that, yhat, gate, upd, qh, do, kv, rstd = call(
        attend_kernel,
        [((ROWS, 8, N), F32)] + [((ROWS, C, N), F32)] * 6 + [((ROWS, 2 * C, N), BF16), ((ROWS, 8, N), F32)],
        [VMEM] * 5 + [SMEM] + [VMEM] * 9,
        [(2, SHARDS * 16, 128)],
    )(
        tri, z, query_pair, cotangent, template_mask, template_mask, row(norm_gain), gate_weight, out_weight,
        row(tri_gain), row(pair_gain), kv_weight, row(query_gain), query_weight, attn_out_weight,
    )
    sg = lax.all_gather(sg, "tmpl")
    dtri, dln, dzin, dqh = call(
        back_kernel,
        [((SHARDS, 16, N), BF16), ((ROWS, C, N), F32), ((ROWS, C, N), F32), ((ROWS, C, N), BF16)],
        [VMEM] * 10 + [SMEM] + [VMEM] * 5,
        [(2, SHARDS * 16, 128)],
    )(
        sg, that, yhat, gate, upd, qh, do, kv, rstd, template_mask, template_mask, gate_weight, out_weight,
        row(tri_gain), row(pair_gain), kv_weight,
    )
    dtri = every(dtri)
    dqh = dqh + swap(dqh, "tmpl", 4, 1)
    (dlr,) = call(tri_back_kernel, [((SHARDS, 32, N), BF16)], [VMEM, VMEM])(dtri, mats)
    dlr = every(dlr)
    dqh = dqh + swap(dqh, "tmpl", 4, 2)
    grad, proj = call(
        final_kernel,
        [((ROWS, N, C), F32), ((C, 2 * C), F32)],
        [VMEM] * 5 + [SMEM] + [VMEM] * 3,
        [(2, SHARDS * 32, 128)],
    )(dlr, z, dln, dzin, template_mask, template_mask, row(norm_gain), left_weight, right_weight)
    (query_grad,) = call(query_kernel, [((ROWS, N, 2 * C), F32)], [VMEM] * 4)(
        query_pair, dqh, row(query_gain), query_weight
    )
    proj = proj + swap(proj, "tmpl", 4, 1)
    proj = proj + swap(proj, "tmpl", 4, 2)
    proj = jnp.sum(every(jnp.broadcast_to(proj[None], (SHARDS, C, 2 * C))), axis=0)
    return grad[None], query_grad, jnp.stack([proj[:, :C], proj[:, C:]])


def solution(mesh):
    in_specs = (
        P("tmpl", "row", None, None),
        P(),
        P(),
        P("row", None, None),
        *([P()] * 12),
        P("row", None, None),
    )
    out_specs = (P("tmpl", "row", None, None), P("row", None, None), P())
    return jax.shard_map(local, mesh=mesh, in_specs=in_specs, out_specs=out_specs, check_vma=False)
```

```python
import functools

import jax
import jax.numpy as jnp
from jax import lax
from jax.experimental import pallas as pl
from jax.experimental.pallas import tpu as pltpu
from jax.sharding import PartitionSpec as P

F32 = jnp.float32
BF16 = jnp.bfloat16
HEADS = 4
HEAD_DIM = 16
C = 64
ROWS = 8
N = 256
SHARDS = 32
UNROLL = 4
VMEM = pl.BlockSpec(memory_space=pltpu.VMEM)
SMEM = pl.BlockSpec(memory_space=pltpu.SMEM)


def dot(a, b, contract=((1,), (0,))):
    return lax.dot_general(a, b, (contract, ((), ())), preferred_element_type=F32)


def flip(x):
    return x.astype(F32).T


def column(row, lanes=N):
    tall = jnp.broadcast_to(row, (128, row.shape[1])).T
    return jnp.concatenate([tall] * (lanes // 128), axis=1)


def hat(x):
    mean = jnp.mean(x, 0, keepdims=True)
    cent = x - mean
    var = jnp.mean(cent * cent, 0, keepdims=True)
    rstd = lax.rsqrt(var + 1e-05)
    return cent * rstd, rstd


def hat_back(dy, xhat, rstd):
    return rstd * (dy - jnp.mean(dy, 0, keepdims=True) - xhat * jnp.mean(dy * xhat, 0, keepdims=True))


def put_rows(spread, first, step, x):
    for half in range(2):
        spread[half, pl.ds(first, x.shape[0], stride=step), :] = x[:, 128 * half : 128 * half + 128]


def take_rows(wide, first, step):
    return jnp.concatenate([wide[half, pl.ds(first, SHARDS, stride=step), :] for half in range(2)], axis=1)


def pack(spread, out):
    for half in range(2):
        out[:, :, 128 * half : 128 * half + 128] = spread[half].reshape(out.shape[0], out.shape[1], 128).astype(BF16)


def unpack(x, wide):
    for half in range(2):
        wide[half] = x[:, :, 128 * half : 128 * half + 128].astype(F32).reshape(wide.shape[1], 128)


def place(rows_ref):
    t = lax.axis_index("tmpl")
    start = lax.axis_index("row") * ROWS
    mask_row = rows_ref[pl.ds(t, 1), :].astype(F32)
    return t, start, mask_row


def each_row(body, carry=0, unroll=UNROLL):
    def step(s, carry):
        for u in range(unroll):
            carry = body(s * unroll + u, carry)
        return carry

    if unroll == ROWS:
        return step(0, carry)
    return lax.fori_loop(0, ROWS // unroll, step, carry)


def project_kernel(pair, mask, mask_s, res, res_s, table_t, gain, wl, wr, lr_out, z_out, ln_out, spread):
    t, start, mask_row = place(mask)
    weight = jnp.concatenate([flip(wl[...]), flip(wr[...])], axis=0).astype(BF16)
    table = table_t[...]
    g = column(gain[...])
    residues = res[...]
    bins = lax.broadcasted_iota(jnp.int32, (128, N), 0)

    def body(i, carry):
        offset = jnp.clip(res_s[start + i] - residues, -64, 63) + 64
        onehot = jnp.where(bins == offset, 1.0, 0.0).astype(BF16)
        z = pair[i].astype(F32) + dot(table, onehot)
        z_out[i] = z
        ln_b = (hat(z)[0] * g).astype(BF16)
        ln_out[i] = ln_b
        both = dot(weight, ln_b) * (mask_row * mask_s[t, start + i].astype(F32))
        for q in range(4):
            put_rows(spread, 8 * q + i, 32, both[32 * q : 32 * q + 32])
        return carry

    each_row(body)
    pack(spread, lr_out)


def query_kernel(query, cot, ln_b, wg, q_gain, wq_t, wao, qh_out, do_out, gate_out):
    wg_t = flip(wg[...]).astype(BF16)
    wq_v, wao_v, g_query = wq_t[...], wao[...], q_gain[...]

    def body(i, carry):
        x = query[i].astype(F32)
        cent = x - jnp.mean(x, -1, keepdims=True)
        var = jnp.mean(cent * cent, -1, keepdims=True)
        qn = (cent * lax.rsqrt(var + 1e-05) * g_query).astype(BF16)
        qh_out[i] = dot(wq_v, qn, ((1,), (1,))) * HEAD_DIM ** (-0.5)
        do_out[i] = dot(wao_v, cot[i], ((1,), (1,)))
        gate_out[i] = jax.nn.sigmoid(dot(wg_t, ln_b[i]))
        return carry

    each_row(body)


def tri_kernel(lr, tri_out, mats_out):
    wide = lr[...].astype(F32)
    mats = [wide[:, 8 * q : 8 * q + 8, :].reshape(N, N).astype(BF16) for q in range(4)]
    for q in range(4):
        mats_out[q] = mats[q]
    parts = [dot(mats[cc], mats[2 + cc], ((1,), (1,))).reshape(SHARDS, 8, N) for cc in range(2)]
    tri_out[...] = jnp.concatenate(parts, axis=1).astype(BF16)


def heads_sum(x):
    return jnp.sum(x.reshape(HEADS, HEAD_DIM, N), axis=1)


def heads_spread(x):
    return jnp.broadcast_to(x[:, None, :], (HEADS, HEAD_DIM, N)).reshape(C, N)


def attend_kernel(
    tri, z, qh, do, gate, mask, mask_s, wo, tri_gain, pair_gain, wkv,
    sg_out, that_out, yhat_out, upd_out, kv_out, rstd_out, wide,
):
    t, start, mask_row = place(mask)
    unpack(tri, wide)
    wo_t = flip(wo[...]).astype(BF16)
    wkv_t = flip(wkv[...]).astype(BF16)
    g_tri, g_pair = column(tri_gain[...]), column(pair_gain[...])

    def body(i, carry):
        tri_i = jnp.concatenate([take_rows(wide, i, 16), take_rows(wide, 8 + i, 16)], axis=0)
        that, rstd_t = hat(tri_i)
        upd = dot(wo_t, (that * g_tri).astype(BF16))
        yhat, rstd_y = hat(z[i] + gate[i] * upd)
        kv = dot(wkv_t, (yhat * g_pair).astype(BF16)).astype(BF16)
        kv_f = kv.astype(F32)
        pm = mask_row * mask_s[t, start + i].astype(F32)
        score = heads_sum(qh[i] * kv_f[:C]) * pm + (pm - 1.0) * 1000000000.0
        dot_v = heads_sum(do[i] * kv_f[C:])
        sg_out[i] = jnp.concatenate([score, dot_v], axis=0)
        that_out[i] = that
        yhat_out[i] = yhat
        upd_out[i] = upd
        kv_out[i] = kv
        rstd_out[i] = jnp.concatenate([jnp.broadcast_to(rstd_t, (4, N)), jnp.broadcast_to(rstd_y, (4, N))], axis=0)
        return carry

    each_row(body)


def back_kernel(
    sg, that, yhat, gate, upd, qh, do, rstd, mask, mask_s, wo, tri_gain, pair_gain, wkv,
    dtri_out, ds_out, dy_out, spread,
):
    t, start, mask_row = place(mask)
    g_tri, g_pair = column(tri_gain[...]), column(pair_gain[...])
    wo_v, wkv_v = wo[...], wkv[...]

    def body(i, carry):
        pm = mask_row * mask_s[t, start + i].astype(F32)
        every = [sg[s, i] for s in range(4)]
        own = sg[t, i]
        top = jnp.maximum(jnp.maximum(every[0][:4], every[1][:4]), jnp.maximum(every[2][:4], every[3][:4]))
        expo = [jnp.exp(e[:4] - top) for e in every]
        inv = 1.0 / (expo[0] + expo[1] + expo[2] + expo[3])
        delta = sum(ex * e[4:] for ex, e in zip(expo, every)) * inv
        prob = jnp.exp(own[:4] - top) * inv
        ds_head = pm * prob * (own[4:] - delta)
        ds_out[i] = ds_head
        d_kv = jnp.concatenate([heads_spread(ds_head) * qh[i], heads_spread(prob) * do[i]], axis=0).astype(BF16)
        rs = rstd[i]
        d_y = hat_back(dot(wkv_v, d_kv) * g_pair, yhat[i], rs[4:5])
        dy_out[i] = d_y
        d_tn = dot(wo_v, (d_y * gate[i]).astype(BF16)) * g_tri
        d_tri = hat_back(d_tn, that[i], rs[0:1])
        put_rows(spread, i, 16, d_tri[:32])
        put_rows(spread, 8 + i, 16, d_tri[32:])
        return carry

    each_row(body)
    pack(spread, dtri_out)


def side_kernel(ds, kv, d_y, upd, gate, z, norm_gain, wg, dqh_out, base_out):
    g = column(norm_gain[...])
    wg_v = wg[...]

    def body(i, carry):
        dqh_out[i] = (heads_spread(ds[i]) * kv[i].astype(F32)[:C]).astype(BF16)
        gate_i, d_y_i = gate[i], d_y[i]
        d_gpre = d_y_i * upd[i] * gate_i * (1.0 - gate_i)
        zhat, rstd = hat(z[i])
        base_out[i] = d_y_i + hat_back(dot(wg_v, d_gpre.astype(BF16)) * g, zhat, rstd)
        return carry

    each_row(body)


def tri_back_kernel(dtri, mats, out):
    wide = dtri[...].astype(F32)
    d = [wide[:, 8 * cc : 8 * cc + 8, :].reshape(N, N).astype(BF16) for cc in range(2)]
    parts = [dot(d[cc], mats[2 + cc]) for cc in range(2)]
    parts += [dot(d[cc], mats[cc], ((0,), (0,))) for cc in range(2)]
    out[...] = jnp.concatenate([p.reshape(SHARDS, 8, N) for p in parts], axis=1).astype(BF16)


def weight_kernel(dlr, ln_b, mask, mask_s, proj_out, d_out, wide):
    t, start, mask_row = place(mask)
    unpack(dlr, wide)

    def body(i, total):
        pm = mask_row * mask_s[t, start + i].astype(F32)
        parts = [take_rows(wide, 8 * q + i, 32) for q in range(4)]
        d = (jnp.concatenate(parts, axis=0) * pm).astype(BF16)
        d_out[i] = d
        return total + dot(ln_b[i], d, ((1,), (1,)))

    proj_out[...] = each_row(body, jnp.zeros((C, 2 * C), F32))


def pair_grad_kernel(d, z, base, norm_gain, wl, wr, grad_out):
    g = column(norm_gain[...])
    weight = jnp.concatenate([wl[...], wr[...]], axis=1)

    def body(i, carry):
        zhat, rstd = hat(z[i])
        grad_out[i] = base[i] + hat_back(dot(weight, d[i]) * g, zhat, rstd)
        return carry

    each_row(body)


def query_grad_kernel(query, dqh, dqh_far, gain, wq_t, out):
    g = gain[...] * HEAD_DIM ** (-0.5)
    wq_v = wq_t[...]

    def body(i, carry):
        x = query[i].astype(F32)
        cent = x - jnp.mean(x, -1, keepdims=True)
        var = jnp.mean(cent * cent, -1, keepdims=True)
        rstd = lax.rsqrt(var + 1e-05)
        xhat = cent * rstd
        both = (dqh[i].astype(F32) + dqh_far[i].astype(F32)).astype(BF16)
        dy = dot(both, wq_v, ((0,), (0,))) * g
        out[i] = rstd * (dy - jnp.mean(dy, -1, keepdims=True) - xhat * jnp.mean(dy * xhat, -1, keepdims=True))
        return carry

    each_row(body)


def sum_kernel(parts, out):
    total = jnp.sum(parts[...].astype(F32), axis=0)
    out[0] = total[:, :C]
    out[1] = total[:, C:]


def call(kernel, outs, specs, scratch=(), us=3):
    return pl.pallas_call(
        kernel,
        out_shape=[jax.ShapeDtypeStruct(s, d) for s, d in outs],
        in_specs=specs,
        out_specs=[VMEM] * len(outs),
        scratch_shapes=[pltpu.VMEM(s, F32) for s in scratch],
        compiler_params=pltpu.CompilerParams(vmem_limit_bytes=40 * 1024 * 1024),
        cost_estimate=pl.CostEstimate(flops=us * 10**9, bytes_accessed=us * 3 * 10**6, transcendentals=0),
    )


def swap(x, bit):
    return lax.ppermute(x, "tmpl", [(i, i ^ bit) for i in range(4)])


def after(x, *others):
    return lax.optimization_barrier((x, *others))


def local(
    template_pair, template_mask, residue_index, query_pair, relpos_table, norm_gain, left_weight, right_weight,
    gate_weight, out_weight, tri_gain, pair_gain, kv_weight, query_gain, query_weight, attn_out_weight, cotangent,
):
    pair = jnp.swapaxes(template_pair[0], 1, 2)
    row = lambda x: x.reshape(1, -1)
    every = functools.partial(lax.all_to_all, axis_name="row", split_axis=0, concat_axis=0, tiled=True)
    plane, half = (ROWS, C, N), (ROWS, 2 * C, N)
    masks = (template_mask, template_mask)
    lr, z, ln_b = call(
        project_kernel,
        [((SHARDS, 32, N), BF16), (plane, F32), (plane, BF16)],
        [VMEM, VMEM, SMEM, VMEM, SMEM] + [VMEM] * 4,
        [(2, SHARDS * 32, 128)],
    )(
        pair, *masks, row(residue_index), residue_index, relpos_table.T, row(norm_gain), left_weight, right_weight,
    )
    lr_all = every(lr)
    qh, do, gate = call(query_kernel, [(plane, F32)] * 3, [VMEM] * 7)(
        query_pair, cotangent, ln_b, gate_weight, row(query_gain), query_weight.T, attn_out_weight
    )
    lr_all, qh, do, gate = after(lr_all, qh, do, gate)
    tri, mats = call(tri_kernel, [((SHARDS, 16, N), BF16), ((4, N, N), BF16)], [VMEM], us=1)(lr_all)
    tri = every(tri)
    sg, that, yhat, upd, kv, rstd = call(
        attend_kernel,
        [((ROWS, 8, N), F32)] + [(plane, F32)] * 3 + [(half, BF16), ((ROWS, 8, N), F32)],
        [VMEM] * 6 + [SMEM] + [VMEM] * 4,
        [(2, SHARDS * 16, 128)],
    )(tri, z, qh, do, gate, *masks, out_weight, row(tri_gain), row(pair_gain), kv_weight)
    sg = lax.all_gather(sg, "tmpl")
    dtri, ds, d_y = call(
        back_kernel,
        [((SHARDS, 16, N), BF16), ((ROWS, HEADS, N), F32), (plane, F32)],
        [VMEM] * 9 + [SMEM] + [VMEM] * 4,
        [(2, SHARDS * 16, 128)],
    )(sg, that, yhat, gate, upd, qh, do, rstd, *masks, out_weight, row(tri_gain), row(pair_gain), kv_weight)
    dtri = every(dtri)
    dqh, base = call(side_kernel, [(plane, BF16), (plane, F32)], [VMEM] * 8)(
        ds, kv, d_y, upd, gate, z, row(norm_gain), gate_weight
    )
    dqh = dqh + swap(dqh, 1)
    dtri, dqh, base = after(dtri, dqh, base)
    (dlr,) = call(tri_back_kernel, [((SHARDS, 32, N), BF16)], [VMEM, VMEM], us=1)(dtri, mats)
    dlr = every(dlr)
    dqh_far = swap(dqh, 2)
    dlr, dqh_far = after(dlr, dqh_far)
    proj, d = call(
        weight_kernel,
        [((C, 2 * C), F32), (half, BF16)],
        [VMEM] * 3 + [SMEM],
        [(2, SHARDS * 32, 128)],
    )(dlr, ln_b, *masks)
    near = swap(proj, 1)
    (grad,) = call(pair_grad_kernel, [(plane, F32)], [VMEM] * 6)(d, z, base, row(norm_gain), left_weight, right_weight)
    proj = proj + near
    proj = (proj + swap(proj, 2)).astype(BF16)
    parts = every(jnp.broadcast_to(proj[None], (SHARDS, C, 2 * C)))
    (query_grad,) = call(query_grad_kernel, [((ROWS, N, 2 * C), F32)], [VMEM] * 5)(
        query_pair, dqh, dqh_far, row(query_gain), query_weight.T
    )
    parts, query_grad = after(parts, query_grad)
    (proj,) = call(sum_kernel, [((2, C, C), F32)], [VMEM], us=1)(parts)
    return jnp.swapaxes(grad, 1, 2)[None], query_grad, proj


def solution(mesh):
    in_specs = (
        P("tmpl", "row", None, None),
        P(),
        P(),
        P("row", None, None),
        *([P()] * 12),
        P("row", None, None),
    )
    out_specs = (P("tmpl", "row", None, None), P("row", None, None), P())
    return jax.shard_map(local, mesh=mesh, in_specs=in_specs, out_specs=out_specs, check_vma=False)
```

```python
import functools

import jax
import jax.numpy as jnp
from jax import lax
from jax.experimental import pallas as pl
from jax.experimental.pallas import tpu as pltpu
from jax.sharding import PartitionSpec as P

F32 = jnp.float32
BF16 = jnp.bfloat16
HEADS = 4
HEAD_DIM = 16
C = 64
ROWS = 8
N = 256
SHARDS = 32
UNROLL = 4
HALF = ROWS // 2
ANY = pl.BlockSpec(memory_space=pltpu.HBM)
VMEM = pl.BlockSpec(memory_space=pltpu.VMEM)


def dot(a, b, contract=((1,), (0,))):
    return lax.dot_general(a, b, (contract, ((), ())), preferred_element_type=F32)


def flip(x):
    return x.astype(F32).T


def column(row):
    return jnp.broadcast_to(row, (128, row.shape[1])).T


def twice(x):
    return jnp.concatenate([x, x], axis=1)


def slab(weights, n, width=C):
    return weights[:, 128 * n : 128 * n + width]


def hat(x):
    mean = jnp.mean(x, 0, keepdims=True)
    cent = x - mean
    var = jnp.mean(cent * cent, 0, keepdims=True)
    rstd = lax.rsqrt(var + 1e-05)
    return cent * rstd, rstd


def hat_back(dy, xhat, rstd):
    return rstd * (dy - jnp.mean(dy, 0, keepdims=True) - xhat * jnp.mean(dy * xhat, 0, keepdims=True))


def put_rows(spread, first, step, x):
    for half in range(2):
        spread[half, pl.ds(first, x.shape[0], stride=step), :] = x[:, 128 * half : 128 * half + 128]


def take_rows(wide, first, step):
    return jnp.concatenate([wide[half, pl.ds(first, SHARDS, stride=step), :] for half in range(2)], axis=1)


def pack(spread, out):
    for half in range(2):
        out[:, :, 128 * half : 128 * half + 128] = spread[half].reshape(out.shape[0], out.shape[1], 128).astype(BF16)


def unpack(x, wide):
    for half in range(2):
        wide[half] = x[:, :, 128 * half : 128 * half + 128].astype(F32).reshape(wide.shape[1], 128)


def place(rows_ref):
    t = lax.axis_index("tmpl")
    start = lax.axis_index("row") * ROWS
    mask_row = rows_ref[pl.ds(t, 1), :].astype(F32)
    return t, start, mask_row


def each_row(body, carry=0, rows=ROWS, unroll=UNROLL):
    def step(s, carry):
        for u in range(unroll):
            carry = body(s * unroll + u, carry)
        return carry

    if unroll == rows:
        return step(0, carry)
    return lax.fori_loop(0, rows // unroll, step, carry)


def fetch(sources, places, sems):
    copies = [pltpu.make_async_copy(src, dst, sems.at[n]) for n, (src, dst) in enumerate(zip(sources, places))]
    for copy in copies:
        copy.start()
    for copy in copies:
        copy.wait()


def relative(res_s, residues, table, at):
    bins = lax.broadcasted_iota(jnp.int32, (128, N), 0)
    offset = jnp.clip(res_s[at] - residues, -64, 63) + 64
    return dot(table, jnp.where(bins == offset, 1.0, 0.0).astype(BF16))


def project_kernel(*refs):
    sources, outs, (spread, sems), places = refs[:14], refs[14:19], refs[19:21], refs[21:]
    lr_out, z_out, pm_out, weights_out, gains_out = outs
    fetch(sources, places, sems)
    pair, res, res_s, table_t, mask, mask_s, wl, wr, wg, wo, wkv, norm_gain, tri_gain, pair_gain = places
    t, start, mask_row = place(mask)
    weight = jnp.concatenate([flip(wl[...]), flip(wr[...])], axis=0).astype(BF16)
    table, residues, gain = table_t[...], res[...], column(norm_gain[...])
    g = twice(gain)

    def body(i, carry):
        z = pair[i].astype(F32) + relative(res_s, residues, table, start + i)
        z_out[i] = z
        pm = mask_row * mask_s[t, start + i].astype(F32)
        pm_out[i] = pm
        both = dot(weight, (hat(z)[0] * g).astype(BF16)) * pm
        for q in range(4):
            put_rows(spread, 8 * q + i, 32, both[32 * q : 32 * q + 32])
        return carry

    each_row(body)
    pack(spread, lr_out)
    blank = jnp.zeros((C, C), BF16)
    wkv_t = flip(wkv[...]).astype(BF16)
    parts = [wkv[...], wl[...], wr[...], flip(wo[...]).astype(BF16), blank, wo[...], blank, wg[...], blank]
    parts += [wkv_t[:C], blank, wkv_t[C:], blank, flip(wg[...]).astype(BF16), blank]
    weights_out[...] = jnp.concatenate(parts, axis=1)
    gains_out[0] = gain
    gains_out[1] = column(tri_gain[...])
    gains_out[2] = column(pair_gain[...])


def prepare_kernel(z, weights, gains, query, cot, q_gain, wq_t, wao, ln_out, qh_out, do_out, gate_out):
    wg_t, g = slab(weights, 7), twice(gains[0])
    wq_v, wao_v, g_query = wq_t[...], wao[...], q_gain[...]

    def body(i, carry):
        ln_b = (hat(z[i])[0] * g).astype(BF16)
        ln_out[i] = ln_b
        x = query[i].astype(F32)
        cent = x - jnp.mean(x, -1, keepdims=True)
        var = jnp.mean(cent * cent, -1, keepdims=True)
        qn = (cent * lax.rsqrt(var + 1e-05) * g_query).astype(BF16)
        qh_out[i] = dot(wq_v, qn, ((1,), (1,))) * HEAD_DIM ** (-0.5)
        do_out[i] = dot(wao_v, cot[i], ((1,), (1,)))
        gate_out[i] = jax.nn.sigmoid(dot(wg_t, ln_b))
        return carry

    each_row(body)


def tri_kernel(lr, tri_out, mats_out):
    wide = lr[...].astype(F32)
    mats = [wide[:, 8 * q : 8 * q + 8, :].reshape(N, N).astype(BF16) for q in range(4)]
    for q in range(4):
        mats_out[q] = mats[q]
    parts = [dot(mats[cc], mats[2 + cc], ((1,), (1,))).reshape(SHARDS, 8, N) for cc in range(2)]
    tri_out[...] = jnp.concatenate(parts, axis=1).astype(BF16)


def heads_sum(x):
    return jnp.sum(x.reshape(HEADS, HEAD_DIM, N), axis=1)


def heads_spread(x):
    return jnp.broadcast_to(x[:, None, :], (HEADS, HEAD_DIM, N)).reshape(C, N)


def attend_kernel(
    tri, z, qh, do, gate, pm, weights, gains, sg_out, that_out, yhat_out, upd_out, kv_out, rstd_out, wide
):
    unpack(tri, wide)
    wo_t = slab(weights, 2)
    wkv_t = jnp.concatenate([slab(weights, 5), slab(weights, 6)], axis=0)
    g_tri, g_pair = twice(gains[1]), twice(gains[2])

    def body(i, carry):
        tri_i = jnp.concatenate([take_rows(wide, i, 16), take_rows(wide, 8 + i, 16)], axis=0)
        that, rstd_t = hat(tri_i)
        upd = dot(wo_t, (that * g_tri).astype(BF16))
        yhat, rstd_y = hat(z[i] + gate[i] * upd)
        kv = dot(wkv_t, (yhat * g_pair).astype(BF16)).astype(BF16)
        kv_f = kv.astype(F32)
        score = heads_sum(qh[i] * kv_f[:C]) * pm[i] + (pm[i] - 1.0) * 1000000000.0
        dot_v = heads_sum(do[i] * kv_f[C:])
        sg_out[i] = jnp.concatenate([score, dot_v], axis=0)
        that_out[i] = that
        yhat_out[i] = yhat
        upd_out[i] = upd
        kv_out[i] = kv
        rstd_out[i] = jnp.concatenate([jnp.broadcast_to(rstd_t, (4, N)), jnp.broadcast_to(rstd_y, (4, N))], axis=0)
        return carry

    each_row(body)


def back_kernel(
    sg, that, yhat, gate, upd, qh, do, kv, rstd, pm, z, weights, gains,
    dtri_out, keep_out, send_out, base_out, spread,
):
    t = lax.axis_index("tmpl")
    core = t % 2
    g_norm, g_tri, g_pair = twice(gains[0]), twice(gains[1]), twice(gains[2])
    wkv_v, wo_v, wg_v = slab(weights, 0, 2 * C), slab(weights, 3), slab(weights, 4)

    def row(i, dqh_out, n):
        every = [sg[s, i] for s in range(4)]
        own = sg[t, i]
        top = jnp.maximum(jnp.maximum(every[0][:4], every[1][:4]), jnp.maximum(every[2][:4], every[3][:4]))
        expo = [jnp.exp(e[:4] - top) for e in every]
        inv = 1.0 / (expo[0] + expo[1] + expo[2] + expo[3])
        delta = sum(ex * e[4:] for ex, e in zip(expo, every)) * inv
        prob = jnp.exp(own[:4] - top) * inv
        ds = heads_spread(pm[i] * prob * (own[4:] - delta))
        dqh_out[n] = (ds * kv[i].astype(F32)[:C]).astype(BF16)
        d_kv = jnp.concatenate([ds * qh[i], heads_spread(prob) * do[i]], axis=0).astype(BF16)
        rs = rstd[i]
        d_y = hat_back(dot(wkv_v, d_kv) * g_pair, yhat[i], rs[4:5])
        gate_i = gate[i]
        d_upd = d_y * gate_i
        d_gate = (d_upd * upd[i] * (1.0 - gate_i)).astype(BF16)
        zhat, rstd_z = hat(z[i])
        base_out[i] = d_y + hat_back(dot(wg_v, d_gate) * g_norm, zhat, rstd_z)
        d_tri = hat_back(dot(wo_v, d_upd.astype(BF16)) * g_tri, that[i], rs[0:1])
        put_rows(spread, i, 16, d_tri[:32])
        put_rows(spread, 8 + i, 16, d_tri[32:])

    def body(n, carry):
        row(core * HALF + n, keep_out, n)
        row((1 - core) * HALF + n, send_out, n)
        return carry

    each_row(body, rows=HALF, unroll=UNROLL // 2)
    pack(spread, dtri_out)


def tri_back_kernel(dtri, mats, out):
    wide = dtri[...].astype(F32)
    d = [wide[:, 8 * cc : 8 * cc + 8, :].reshape(N, N).astype(BF16) for cc in range(2)]
    parts = [dot(d[cc], mats[2 + cc]) for cc in range(2)]
    parts += [dot(d[cc], mats[cc], ((0,), (0,))) for cc in range(2)]
    out[...] = jnp.concatenate([p.reshape(SHARDS, 8, N) for p in parts], axis=1).astype(BF16)


def weight_kernel(dlr, ln_b, pm, proj_out, d_out, wide):
    unpack(dlr, wide)

    def body(i, total):
        parts = [take_rows(wide, 8 * q + i, 32) for q in range(4)]
        d = (jnp.concatenate(parts, axis=0) * pm[i]).astype(BF16)
        d_out[i] = d
        return total + dot(ln_b[i], d, ((1,), (1,)))

    proj_out[...] = each_row(body, jnp.zeros((C, 2 * C), F32))


def pair_grad_kernel(d, z, base, weights, gains, grad_out):
    g = twice(gains[0])
    weight = slab(weights, 1, 2 * C)

    def body(i, carry):
        zhat, rstd = hat(z[i])
        grad_out[i] = base[i] + hat_back(dot(weight, d[i]) * g, zhat, rstd)
        return carry

    each_row(body)


def query_grad_kernel(own, other, query_h, gain_h, wq_h, out, sems, query, gain, wq_t):
    fetch((query_h, gain_h, wq_h), (query, gain, wq_t), sems)
    core = lax.axis_index("tmpl") % 2
    g = gain[...] * HEAD_DIM ** (-0.5)
    wq_v = wq_t[...]

    def body(i, d_qh):
        x = query[i].astype(F32)
        cent = x - jnp.mean(x, -1, keepdims=True)
        var = jnp.mean(cent * cent, -1, keepdims=True)
        rstd = lax.rsqrt(var + 1e-05)
        xhat = cent * rstd
        dy = dot(d_qh, wq_v, ((0,), (0,))) * g
        out[i] = rstd * (dy - jnp.mean(dy, -1, keepdims=True) - xhat * jnp.mean(dy * xhat, -1, keepdims=True))

    for i in range(HALF):
        body(core * HALF + i, own[i])
        body((1 - core) * HALF + i, other[i])


def fan_kernel(own, far, out):
    total = (own[...] + far[...]).astype(BF16)
    for s in range(SHARDS):
        out[s] = total


def sum_kernel(parts, out):
    total = jnp.sum(parts[...].astype(F32), axis=0)
    out[0] = total[:, :C]
    out[1] = total[:, C:]


def call(kernel, outs, specs, scratch=(), vmem=40):
    return pl.pallas_call(
        kernel,
        out_shape=[jax.ShapeDtypeStruct(s, d) for s, d in outs],
        in_specs=specs,
        out_specs=[VMEM] * len(outs),
        scratch_shapes=list(scratch),
        compiler_params=pltpu.CompilerParams(vmem_limit_bytes=vmem * 1024 * 1024),
    )


def wide_scratch(rows):
    return pltpu.VMEM((2, rows, 128), F32)


def fetched(*arrays):
    return [pltpu.SemaphoreType.DMA((len(arrays),))] + [pltpu.VMEM(a.shape, a.dtype) for a in arrays]


def swap(x, bit):
    return lax.ppermute(x, "tmpl", [(i, i ^ bit) for i in range(4)])


def after(x, *others):
    return lax.optimization_barrier((x, *others))


def local(
    template_pair, template_mask, residue_index, query_pair, relpos_table, norm_gain, left_weight, right_weight,
    gate_weight, out_weight, tri_gain, pair_gain, kv_weight, query_gain, query_weight, attn_out_weight, cotangent,
):
    pair = jnp.swapaxes(template_pair[0], 1, 2)
    row = lambda x: x.reshape(1, -1)
    every = functools.partial(lax.all_to_all, axis_name="row", split_axis=0, concat_axis=0, tiled=True)
    plane, half = (ROWS, C, N), (ROWS, 2 * C, N)
    sources = (
        pair, row(residue_index), residue_index, relpos_table.T, template_mask, template_mask, left_weight,
        right_weight, gate_weight, out_weight, kv_weight, row(norm_gain), row(tri_gain), row(pair_gain),
    )
    scratch = fetched(*sources)
    for n in (2, 5):
        scratch[1 + n] = pltpu.SMEM(sources[n].shape, sources[n].dtype)
    lr, z, pm, weights, gains = call(
        project_kernel,
        [((SHARDS, 32, N), BF16), (plane, F32), ((ROWS, 1, N), F32), ((C, 8 * 128), BF16), ((3, C, 128), F32)],
        [ANY] * 14,
        [wide_scratch(SHARDS * 32)] + scratch,
        vmem=62,
    )(*sources)
    lr_all = every(lr)
    prepared = call(prepare_kernel, [(plane, BF16)] + [(plane, F32)] * 3, [VMEM] * 8)(
        z, weights, gains, query_pair, cotangent, row(query_gain), query_weight.T, attn_out_weight
    )
    lr_all, ln_b, qh, do, gate = after(lr_all, *prepared)
    tri, mats = call(tri_kernel, [((SHARDS, 16, N), BF16), ((4, N, N), BF16)], [VMEM])(lr_all)
    tri = every(tri)
    sg, that, yhat, upd, kv, rstd = call(
        attend_kernel,
        [((ROWS, 8, N), F32)] + [(plane, F32)] * 3 + [(half, BF16), ((ROWS, 8, N), F32)],
        [VMEM] * 8,
        [wide_scratch(SHARDS * 16)],
    )(tri, z, qh, do, gate, pm, weights, gains)
    sg = lax.all_gather(sg, "tmpl")
    dtri, keep, send, base = call(
        back_kernel,
        [((SHARDS, 16, N), BF16)] + [((HALF, C, N), BF16)] * 2 + [(plane, F32)],
        [VMEM] * 13,
        [wide_scratch(SHARDS * 16)],
    )(sg, that, yhat, gate, upd, qh, do, kv, rstd, pm, z, weights, gains)
    dtri, keep = after(dtri, keep + swap(send, 1))
    dtri = every(dtri)
    (dlr,) = call(tri_back_kernel, [((SHARDS, 32, N), BF16)], [VMEM, VMEM])(dtri, mats)
    dlr, keep = after(every(dlr), keep)
    proj, d = call(
        weight_kernel, [((C, 2 * C), F32), (half, BF16)], [VMEM] * 3, [wide_scratch(SHARDS * 32)]
    )(dlr, ln_b, pm)
    near = swap(proj, 1)
    (grad,) = call(pair_grad_kernel, [(plane, F32)], [VMEM] * 5)(d, z, base, weights, gains)
    proj = proj + near
    (fan,) = call(fan_kernel, [((SHARDS, C, 2 * C), BF16)], [VMEM] * 2)(proj, swap(proj, 2))
    fan, grad, own = after(fan, grad, keep + swap(keep, 2))
    parts = every(fan)
    sources = (query_pair, row(query_gain), query_weight.T)
    (query_grad,) = call(
        query_grad_kernel, [((ROWS, N, 2 * C), F32)], [VMEM] * 2 + [ANY] * 3, fetched(*sources)
    )(own, swap(own, 1), *sources)
    parts, query_grad = after(parts, query_grad)
    (proj,) = call(sum_kernel, [((2, C, C), F32)], [VMEM])(parts)
    return jnp.swapaxes(grad, 1, 2)[None], query_grad, proj


def solution(mesh):
    in_specs = (
        P("tmpl", "row", None, None),
        P(),
        P(),
        P("row", None, None),
        *([P()] * 12),
        P("row", None, None),
    )
    out_specs = (P("tmpl", "row", None, None), P("row", None, None), P())
    return jax.shard_map(local, mesh=mesh, in_specs=in_specs, out_specs=out_specs, check_vma=False)
```

```python
import functools

import jax
import jax.numpy as jnp
from jax import lax
from jax.experimental import pallas as pl
from jax.experimental.pallas import tpu as pltpu
from jax.sharding import PartitionSpec as P

F32 = jnp.float32
BF16 = jnp.bfloat16
HEADS = 4
HEAD_DIM = 16
C = 64
ROWS = 8
N = 256
SHARDS = 32
UNROLL = 8
HALF = ROWS // 2
ANY = pl.BlockSpec(memory_space=pltpu.HBM)
VMEM = pl.BlockSpec(memory_space=pltpu.VMEM)


def dot(a, b, contract=((1,), (0,))):
    return lax.dot_general(a, b, (contract, ((), ())), preferred_element_type=F32)


def flip(x):
    return x.astype(F32).T


def column(row):
    return jnp.broadcast_to(row, (128, row.shape[1])).T


def twice(x):
    return jnp.concatenate([x, x], axis=1)


def slab(weights, n, width=C):
    return weights[:, 128 * n : 128 * n + width]


def hat(x):
    mean = jnp.mean(x, 0, keepdims=True)
    cent = x - mean
    var = jnp.mean(cent * cent, 0, keepdims=True)
    rstd = lax.rsqrt(var + 1e-05)
    return cent * rstd, rstd


def hat_back(dy, xhat, rstd):
    return rstd * (dy - jnp.mean(dy, 0, keepdims=True) - xhat * jnp.mean(dy * xhat, 0, keepdims=True))


def owner_rows(left, right):
    rows = jnp.concatenate([left, right], axis=0)
    rows = jnp.concatenate([rows, rows], axis=1)
    sub = lax.broadcasted_iota(jnp.int32, (8, 128), 0)
    lane = lax.broadcasted_iota(jnp.int32, (8, 128), 1) // C
    tiles = []
    for pair in range(ROWS // 2):
        mine = (sub == 2 * pair + lane)[None, None]
        spread = jnp.broadcast_to(rows.reshape(4, SHARDS, 1, 128), (4, SHARDS, 8, 128))
        tiles.append(jnp.where(mine, spread, 0.0))
    return tiles


def put_rows(spread, first, step, x):
    for half in range(2):
        spread[half, pl.ds(first, x.shape[0], stride=step), :] = x[:, 128 * half : 128 * half + 128]


def pack(spread, out):
    for half in range(2):
        out[:, :, 128 * half : 128 * half + 128] = spread[half].reshape(out.shape[0], out.shape[1], 128).astype(BF16)


def take_rows(wide, first, step):
    return jnp.concatenate([wide[half, pl.ds(first, SHARDS, stride=step), :] for half in range(2)], axis=1)


def unpack(x, wide):
    for half in range(2):
        wide[half] = x[:, :, 128 * half : 128 * half + 128].astype(F32).reshape(wide.shape[1], 128)


def place(rows_ref):
    t = lax.axis_index("tmpl")
    start = lax.axis_index("row") * ROWS
    mask_row = rows_ref[pl.ds(t, 1), :].astype(F32)
    return t, start, mask_row


def each_row(body, carry=0, rows=ROWS, unroll=UNROLL):
    def step(s, carry):
        for u in range(unroll):
            carry = body(s * unroll + u, carry)
        return carry

    if unroll == rows:
        return step(0, carry)
    return lax.fori_loop(0, rows // unroll, step, carry)


def copies(sources, places, sems, first=0):
    started = [pltpu.make_async_copy(src, dst, sems.at[first + n]) for n, (src, dst) in enumerate(zip(sources, places))]
    for copy in started:
        copy.start()
    return started


def arrive(started):
    for copy in started:
        copy.wait()


def relative(res_s, residues, table, at):
    bins = lax.broadcasted_iota(jnp.int32, (128, N), 0)
    offset = jnp.clip(res_s[at] - residues, -64, 63) + 64
    return dot(table, jnp.where(bins == offset, 1.0, 0.0).astype(BF16))


def project_kernel(*refs):
    sources, outs, places = refs[:14], refs[14:19], refs[28:]
    lhs, normed, lr, z, pm, weights, gains, out_sems, sems = refs[19:28]
    lr_out, z_out, pm_out, weights_out, gains_out = outs
    arriving = copies(sources, places, sems)
    wl, wr, norm_gain, table_t, res, res_s, mask, mask_s, pair, wg, wo, wkv, tri_gain, pair_gain = places
    arrive(arriving[:2])
    for pair_of, tile in enumerate(owner_rows(flip(wl[...]), flip(wr[...]))):
        for q in range(4):
            lhs[:, 8 * q : 8 * q + 8, 128 * pair_of : 128 * pair_of + 128] = tile[q].astype(BF16)
    arrive(arriving[2:9])
    t, start, mask_row = place(mask)
    table, residues, gain = table_t[...], res[...], column(norm_gain[...])
    g = twice(gain)

    def body(i, carry):
        z_i = pair[i].astype(F32) + relative(res_s, residues, table, start + i)
        z[i] = z_i
        pm_i = mask_row * mask_s[t, start + i].astype(F32)
        pm[i] = pm_i
        normed[i * C : i * C + C, :] = (hat(z_i)[0] * g).astype(BF16)
        return carry

    each_row(body)
    both = dot(lhs[...].reshape(SHARDS * 32, ROWS * C), normed[...]).reshape(SHARDS * 4, ROWS, N)
    lr[...] = (both * pm[...].reshape(1, ROWS, N)).reshape(SHARDS, 32, N).astype(BF16)
    leaving = copies((lr, z, pm), (lr_out, z_out, pm_out), out_sems)
    arrive(arriving[9:])
    blank = jnp.zeros((C, C), BF16)
    wkv_t = flip(wkv[...]).astype(BF16)
    parts = [wkv[...], wl[...], wr[...], flip(wo[...]).astype(BF16), blank, wo[...], blank, wg[...], blank]
    parts += [wkv_t[:C], blank, wkv_t[C:], blank, flip(wg[...]).astype(BF16), blank]
    weights[...] = jnp.concatenate(parts, axis=1)
    gains[0] = gain
    gains[1] = column(tri_gain[...])
    gains[2] = column(pair_gain[...])
    leaving += copies((weights, gains), (weights_out, gains_out), out_sems, 3)
    arrive(leaving)


def prepare_kernel(z, weights, gains, query, cot, q_gain, wq_t, wao, ln_out, qh_out, do_out, gate_out):
    wg_t, g = slab(weights, 7), twice(gains[0])
    wq_v, wao_v, g_query = wq_t[...], wao[...], q_gain[...]

    def body(i, carry):
        ln_b = (hat(z[i])[0] * g).astype(BF16)
        ln_out[i] = ln_b
        x = query[i].astype(F32)
        cent = x - jnp.mean(x, -1, keepdims=True)
        var = jnp.mean(cent * cent, -1, keepdims=True)
        qn = (cent * lax.rsqrt(var + 1e-05) * g_query).astype(BF16)
        qh_out[i] = dot(wq_v, qn, ((1,), (1,))) * HEAD_DIM ** (-0.5)
        do_out[i] = dot(wao_v, cot[i], ((1,), (1,)))
        gate_out[i] = jax.nn.sigmoid(dot(wg_t, ln_b))
        return carry

    each_row(body)


def tri_kernel(lr, tri_out, mats_out):
    wide = lr[...].astype(F32)
    mats = [wide[:, 8 * q : 8 * q + 8, :].reshape(N, N).astype(BF16) for q in range(4)]
    for q in range(4):
        mats_out[q] = mats[q]
    parts = [dot(mats[cc], mats[2 + cc], ((1,), (1,))).reshape(SHARDS, 8, N) for cc in range(2)]
    tri_out[...] = jnp.concatenate(parts, axis=1).astype(BF16)


def heads_sum(x):
    return jnp.sum(x.reshape(HEADS, HEAD_DIM, N), axis=1)


def heads_spread(x):
    return jnp.broadcast_to(x[:, None, :], (HEADS, HEAD_DIM, N)).reshape(C, N)


def attend_kernel(
    tri, z, qh, do, gate, pm, weights, gains, sg_out, that_out, yhat_out, upd_out, kv_out, rstd_out, wide
):
    unpack(tri, wide)
    wo_t = slab(weights, 2)
    wkv_t = jnp.concatenate([slab(weights, 5), slab(weights, 6)], axis=0)
    g_tri, g_pair = twice(gains[1]), twice(gains[2])

    def body(i, carry):
        tri_i = jnp.concatenate([take_rows(wide, i, 16), take_rows(wide, 8 + i, 16)], axis=0)
        that, rstd_t = hat(tri_i)
        upd = dot(wo_t, (that * g_tri).astype(BF16))
        yhat, rstd_y = hat(z[i] + gate[i] * upd)
        kv = dot(wkv_t, (yhat * g_pair).astype(BF16)).astype(BF16)
        kv_f = kv.astype(F32)
        score = heads_sum(qh[i] * kv_f[:C]) * pm[i] + (pm[i] - 1.0) * 1000000000.0
        dot_v = heads_sum(do[i] * kv_f[C:])
        sg_out[i] = jnp.concatenate([score, dot_v], axis=0)
        that_out[i] = that
        yhat_out[i] = yhat
        upd_out[i] = upd
        kv_out[i] = kv
        rstd_out[i] = jnp.concatenate([jnp.broadcast_to(rstd_t, (4, N)), jnp.broadcast_to(rstd_y, (4, N))], axis=0)
        return carry

    each_row(body)


def back_kernel(
    sg, that, yhat, gate, upd, qh, do, kv, rstd, pm, weights, gains,
    dtri_out, dqh_out, dy_out, dgate_out, spread,
):
    t = lax.axis_index("tmpl")
    core = t % 2
    g_tri, g_pair = twice(gains[1]), twice(gains[2])
    wkv_v, wo_v = slab(weights, 0, 2 * C), slab(weights, 3)

    def row(i, n):
        every = [sg[s, i] for s in range(4)]
        own = sg[t, i]
        top = jnp.maximum(jnp.maximum(every[0][:4], every[1][:4]), jnp.maximum(every[2][:4], every[3][:4]))
        expo = [jnp.exp(e[:4] - top) for e in every]
        inv = 1.0 / (expo[0] + expo[1] + expo[2] + expo[3])
        delta = sum(ex * e[4:] for ex, e in zip(expo, every)) * inv
        prob = jnp.exp(own[:4] - top) * inv
        ds = heads_spread(pm[i] * prob * (own[4:] - delta))
        dqh_out[n] = (ds * kv[i].astype(F32)[:C]).astype(BF16)
        d_kv = jnp.concatenate([ds * qh[i], heads_spread(prob) * do[i]], axis=0).astype(BF16)
        rs = rstd[i]
        d_y = hat_back(dot(wkv_v, d_kv) * g_pair, yhat[i], rs[4:5])
        gate_i = gate[i]
        d_upd = d_y * gate_i
        d_gate = (d_upd * upd[i] * (1.0 - gate_i)).astype(BF16)
        dy_out[i] = d_y
        dgate_out[i] = d_gate
        d_tri = hat_back(dot(wo_v, d_upd.astype(BF16)) * g_tri, that[i], rs[0:1])
        put_rows(spread, i, 16, d_tri[:32])
        put_rows(spread, 8 + i, 16, d_tri[32:])

    def body(n, carry):
        row(core * HALF + n, n)
        row((1 - core) * HALF + n, HALF + n)
        return carry

    each_row(body, rows=HALF, unroll=UNROLL // 2)
    pack(spread, dtri_out)


def tri_back_kernel(dtri, mats, dqh, near, out, keep_out):
    keep_out[...] = (dqh[:HALF].astype(F32) + near[HALF:].astype(F32)).astype(BF16)
    wide = dtri[...].astype(F32)
    d = [wide[:, 8 * cc : 8 * cc + 8, :].reshape(N, N).astype(BF16) for cc in range(2)]
    parts = [dot(d[cc], mats[2 + cc]) for cc in range(2)]
    parts += [dot(d[cc], mats[cc], ((0,), (0,))) for cc in range(2)]
    out[...] = jnp.concatenate([p.reshape(SHARDS, 8, N) for p in parts], axis=1).astype(BF16)


def weight_kernel(dlr, ln_b, pm, proj_out, d_out, wide):
    unpack(dlr, wide)

    def body(i, total):
        parts = [take_rows(wide, 8 * q + i, 32) for q in range(4)]
        d = (jnp.concatenate(parts, axis=0) * pm[i]).astype(BF16)
        d_out[i] = d
        return total + dot(ln_b[i], d, ((1,), (1,)))

    proj_out[...] = each_row(body, jnp.zeros((C, 2 * C), F32))


def pair_grad_kernel(d, z, d_y, d_gate, weights, gains, grad_out):
    g = twice(gains[0])
    weight = jnp.concatenate([slab(weights, 1, 2 * C), slab(weights, 4)], axis=1)

    def body(i, carry):
        zhat, rstd = hat(z[i])
        d_ln = dot(weight, jnp.concatenate([d[i], d_gate[i]], axis=0))
        grad_out[i] = d_y[i] + hat_back(d_ln * g, zhat, rstd)
        return carry

    each_row(body)


def query_grad_kernel(own, other, query_h, gain_h, wq_h, out, sems, query, gain, wq_t):
    arrive(copies((query_h, gain_h, wq_h), (query, gain, wq_t), sems))
    core = lax.axis_index("tmpl") % 2
    g = gain[...] * HEAD_DIM ** (-0.5)
    wq_v = wq_t[...]

    def body(i, d_qh):
        x = query[i].astype(F32)
        cent = x - jnp.mean(x, -1, keepdims=True)
        var = jnp.mean(cent * cent, -1, keepdims=True)
        rstd = lax.rsqrt(var + 1e-05)
        xhat = cent * rstd
        dy = dot(d_qh, wq_v, ((0,), (0,))) * g
        out[i] = rstd * (dy - jnp.mean(dy, -1, keepdims=True) - xhat * jnp.mean(dy * xhat, -1, keepdims=True))

    for i in range(HALF):
        body(core * HALF + i, own[i])
        body((1 - core) * HALF + i, other[i])


def fan_kernel(own, far, out):
    total = (own[...] + far[...]).astype(BF16)
    for s in range(SHARDS):
        out[s] = total


def sum_kernel(parts, out):
    total = jnp.sum(parts[...].astype(F32), axis=0)
    out[0] = total[:, :C]
    out[1] = total[:, C:]


def call(kernel, outs, specs, scratch=(), vmem=40, home=VMEM):
    return pl.pallas_call(
        kernel,
        out_shape=[jax.ShapeDtypeStruct(s, d) for s, d in outs],
        in_specs=specs,
        out_specs=[home] * len(outs),
        scratch_shapes=list(scratch),
        compiler_params=pltpu.CompilerParams(vmem_limit_bytes=vmem * 1024 * 1024),
    )


def wide_scratch(rows):
    return pltpu.VMEM((2, rows, 128), F32)


def fetched(*arrays):
    return [pltpu.SemaphoreType.DMA((len(arrays),))] + [pltpu.VMEM(a.shape, a.dtype) for a in arrays]


def swap(x, bit):
    return lax.ppermute(x, "tmpl", [(i, i ^ bit) for i in range(4)])


def after(x, *others):
    return lax.optimization_barrier((x, *others))


def local(
    template_pair, template_mask, residue_index, query_pair, relpos_table, norm_gain, left_weight, right_weight,
    gate_weight, out_weight, tri_gain, pair_gain, kv_weight, query_gain, query_weight, attn_out_weight, cotangent,
):
    pair = jnp.swapaxes(template_pair[0], 1, 2)
    row = lambda x: x.reshape(1, -1)
    every = functools.partial(lax.all_to_all, axis_name="row", split_axis=0, concat_axis=0, tiled=True)
    plane, half = (ROWS, C, N), (ROWS, 2 * C, N)
    sources = (
        left_weight, right_weight, row(norm_gain), relpos_table.T, row(residue_index), residue_index, template_mask,
        template_mask, pair, gate_weight, out_weight, kv_weight, row(tri_gain), row(pair_gain),
    )
    scratch = fetched(*sources)
    for n in (5, 7):
        scratch[1 + n] = pltpu.SMEM(sources[n].shape, sources[n].dtype)
    outs = [((SHARDS, 32, N), BF16), (plane, F32), ((ROWS, 1, N), F32), ((C, 8 * 128), BF16), ((3, C, 128), F32)]
    held = [pltpu.VMEM(*o) for o in outs] + [pltpu.SemaphoreType.DMA((len(outs),))]
    lr, z, pm, weights, gains = call(
        project_kernel,
        outs,
        [ANY] * 14,
        [pltpu.VMEM((SHARDS, 32, ROWS * C), BF16), pltpu.VMEM((ROWS * C, N), BF16)] + held + scratch,
        vmem=62,
        home=ANY,
    )(*sources)
    lr_all = every(lr)
    prepared = call(prepare_kernel, [(plane, BF16)] + [(plane, F32)] * 3, [VMEM] * 8)(
        z, weights, gains, query_pair, cotangent, row(query_gain), query_weight.T, attn_out_weight
    )
    lr_all, ln_b, qh, do, gate = after(lr_all, *prepared)
    tri, mats = call(tri_kernel, [((SHARDS, 16, N), BF16), ((4, N, N), BF16)], [VMEM])(lr_all)
    tri = every(tri)
    sg, that, yhat, upd, kv, rstd = call(
        attend_kernel,
        [((ROWS, 8, N), F32)] + [(plane, F32)] * 3 + [(half, BF16), ((ROWS, 8, N), F32)],
        [VMEM] * 8,
        [wide_scratch(SHARDS * 16)],
    )(tri, z, qh, do, gate, pm, weights, gains)
    sg = lax.all_gather(sg, "tmpl")
    dtri, dqh, d_y, d_gate = call(
        back_kernel,
        [((SHARDS, 16, N), BF16), (plane, BF16), (plane, F32), (plane, BF16)],
        [VMEM] * 12,
        [wide_scratch(SHARDS * 16)],
    )(sg, that, yhat, gate, upd, qh, do, kv, rstd, pm, weights, gains)
    dlr, keep = call(tri_back_kernel, [((SHARDS, 32, N), BF16), ((HALF, C, N), BF16)], [VMEM] * 4)(
        every(dtri), mats, dqh, swap(dqh, 1)
    )
    dlr, keep = after(every(dlr), keep)
    proj, d = call(
        weight_kernel, [((C, 2 * C), F32), (half, BF16)], [VMEM] * 3, [wide_scratch(SHARDS * 32)]
    )(dlr, ln_b, pm)
    near = swap(proj, 1)
    (grad,) = call(pair_grad_kernel, [(plane, F32)], [VMEM] * 6)(d, z, d_y, d_gate, weights, gains)
    proj = proj + near
    (fan,) = call(fan_kernel, [((SHARDS, C, 2 * C), BF16)], [VMEM] * 2)(proj, swap(proj, 2))
    fan, grad, own = after(fan, grad, keep + swap(keep, 2))
    parts = every(fan)
    sources = (query_pair, row(query_gain), query_weight.T)
    (query_grad,) = call(
        query_grad_kernel, [((ROWS, N, 2 * C), F32)], [VMEM] * 2 + [ANY] * 3, fetched(*sources)
    )(own, swap(own, 1), *sources)
    parts, query_grad = after(parts, query_grad)
    (proj,) = call(sum_kernel, [((2, C, C), F32)], [VMEM])(parts)
    return jnp.swapaxes(grad, 1, 2)[None], query_grad, proj


def solution(mesh):
    in_specs = (
        P("tmpl", "row", None, None),
        P(),
        P(),
        P("row", None, None),
        *([P()] * 12),
        P("row", None, None),
    )
    out_specs = (P("tmpl", "row", None, None), P("row", None, None), P())
    return jax.shard_map(local, mesh=mesh, in_specs=in_specs, out_specs=out_specs, check_vma=False)
```

```python
import functools

import jax
import jax.numpy as jnp
from jax import lax
from jax.experimental import pallas as pl
from jax.experimental.pallas import tpu as pltpu
from jax.sharding import PartitionSpec as P

F32 = jnp.float32
BF16 = jnp.bfloat16
HEADS = 4
HEAD_DIM = 16
C = 64
ROWS = 8
N = 256
SHARDS = 32
UNROLL = 8
HALF = ROWS // 2
PIECES = 4
HBM = pl.BlockSpec(memory_space=pltpu.HBM)
VMEM = pl.BlockSpec(memory_space=pltpu.VMEM)


def dot(a, b, contract=((1,), (0,))):
    return lax.dot_general(a, b, (contract, ((), ())), preferred_element_type=F32)


def flip(x):
    return x.astype(F32).T


def column(row):
    return jnp.broadcast_to(row, (128, row.shape[1])).T


def twice(x):
    return jnp.concatenate([x, x], axis=1)


def slab(weights, n, width=C):
    return weights[:, 128 * n : 128 * n + width]


def hat(x):
    mean = jnp.mean(x, 0, keepdims=True)
    cent = x - mean
    var = jnp.mean(cent * cent, 0, keepdims=True)
    rstd = lax.rsqrt(var + 1e-05)
    return cent * rstd, rstd


def hat_back(dy, xhat, rstd):
    return rstd * (dy - jnp.mean(dy, 0, keepdims=True) - xhat * jnp.mean(dy * xhat, 0, keepdims=True))


def owner_rows(left, right):
    rows = jnp.concatenate([left, right], axis=0)
    rows = jnp.concatenate([rows, rows], axis=1)
    sub = lax.broadcasted_iota(jnp.int32, (8, 128), 0)
    lane = lax.broadcasted_iota(jnp.int32, (8, 128), 1) // C
    tiles = []
    for pair in range(ROWS // 2):
        mine = (sub == 2 * pair + lane)[None, None]
        spread = jnp.broadcast_to(rows.reshape(4, SHARDS, 1, 128), (4, SHARDS, 8, 128))
        tiles.append(jnp.where(mine, spread, 0.0))
    return tiles


def put_rows(spread, first, step, x):
    for half in range(2):
        spread[half, pl.ds(first, x.shape[0], stride=step), :] = x[:, 128 * half : 128 * half + 128]


def pack(spread, out):
    for half in range(2):
        rows = spread[half, : out.shape[0] * out.shape[1]]
        out[:, :, 128 * half : 128 * half + 128] = rows.reshape(out.shape[0], out.shape[1], 128).astype(BF16)


def take_rows(wide, first, step):
    return jnp.concatenate([wide[half, pl.ds(first, SHARDS, stride=step), :] for half in range(2)], axis=1)


def unpack(x, wide):
    rows = x.shape[0] * x.shape[1]
    for half in range(2):
        wide[half, :rows] = x[:, :, 128 * half : 128 * half + 128].astype(F32).reshape(rows, 128)


def place(rows_ref):
    t = lax.axis_index("tmpl")
    start = lax.axis_index("row") * ROWS
    mask_row = rows_ref[pl.ds(t, 1), :].astype(F32)
    return t, start, mask_row


def each_row(body, carry=0, rows=ROWS, unroll=UNROLL):
    def step(s, carry):
        for u in range(unroll):
            carry = body(s * unroll + u, carry)
        return carry

    if unroll == rows:
        return step(0, carry)
    return lax.fori_loop(0, rows // unroll, step, carry)


def copies(sources, places, sems, first=0):
    started = [pltpu.make_async_copy(src, dst, sems.at[first + n]) for n, (src, dst) in enumerate(zip(sources, places))]
    for copy in started:
        copy.start()
    return started


def arrive(started):
    for copy in started:
        copy.wait()


def relative(res_s, residues, table, at):
    bins = lax.broadcasted_iota(jnp.int32, (128, N), 0)
    offset = jnp.clip(res_s[at] - residues, -64, 63) + 64
    return dot(table, jnp.where(bins == offset, 1.0, 0.0).astype(BF16))


def project_kernel(*refs):
    sources, outs, places = refs[:14], refs[14:19], refs[22:]
    lhs, normed, sems = refs[19:22]
    lr, z, pm, weights, gains = outs
    arriving = copies(sources, places, sems)
    wl, wr, norm_gain, table_t, res, res_s, mask, mask_s, pair, wg, wo, wkv, tri_gain, pair_gain = places
    arrive(arriving[:2])
    for pair_of, tile in enumerate(owner_rows(flip(wl[...]), flip(wr[...]))):
        for side in range(2):
            both = jnp.concatenate([tile[2 * side], tile[2 * side + 1]], axis=1)
            lhs[:, 16 * side : 16 * side + 16, 128 * pair_of : 128 * pair_of + 128] = both.astype(BF16)
    arrive(arriving[2:9])
    t, start, mask_row = place(mask)
    table, residues, gain = table_t[...], res[...], column(norm_gain[...])
    g = twice(gain)

    def body(i, carry):
        z_i = pair[i].astype(F32) + relative(res_s, residues, table, start + i)
        z[i] = z_i
        pm_i = mask_row * mask_s[t, start + i].astype(F32)
        pm[i] = pm_i
        normed[i * C : i * C + C, :] = (hat(z_i)[0] * g).astype(BF16)
        return carry

    each_row(body)
    arrive(arriving[9:])
    blank = jnp.zeros((C, C), BF16)
    wkv_t = flip(wkv[...]).astype(BF16)
    parts = [wkv[...], wl[...], wr[...], flip(wo[...]).astype(BF16), blank, wo[...], blank, wg[...], blank]
    parts += [wkv_t[:C], blank, wkv_t[C:], blank, flip(wg[...]).astype(BF16), blank]
    weights[...] = jnp.concatenate(parts, axis=1)
    gains[0] = gain
    gains[1] = column(tri_gain[...])
    gains[2] = column(pair_gain[...])
    some = SHARDS // PIECES
    for p in range(PIECES):
        owners = slice(p * some, (p + 1) * some)
        both = dot(lhs[owners].reshape(some * 32, ROWS * C), normed[...]).reshape(some * 4, ROWS, N)
        lr[owners] = (both * pm[...].reshape(1, ROWS, N)).reshape(some, 32, N).astype(BF16)


def prepare_kernel(z, weights, gains, query, cot, q_gain, wq_t, wao, ln_out, qh_out, do_out, gate_out):
    wg_t, g = slab(weights, 7), twice(gains[0])
    wq_v, wao_v, g_query = wq_t[...], wao[...], q_gain[...]

    def body(i, carry):
        ln_b = (hat(z[i])[0] * g).astype(BF16)
        ln_out[i] = ln_b
        x = query[i].astype(F32)
        cent = x - jnp.mean(x, -1, keepdims=True)
        var = jnp.mean(cent * cent, -1, keepdims=True)
        qn = (cent * lax.rsqrt(var + 1e-05) * g_query).astype(BF16)
        qh_out[i] = dot(wq_v, qn, ((1,), (1,))) * HEAD_DIM ** (-0.5)
        do_out[i] = dot(wao_v, cot[i], ((1,), (1,)))
        gate_out[i] = jax.nn.sigmoid(dot(wg_t, ln_b))
        return carry

    each_row(body)


def tri_kernel(lr, tri_out, mats_out):
    wide = lr[...].astype(F32)
    mats = [wide[:, 8 * q : 8 * q + 8, :].reshape(N, N).astype(BF16) for q in range(4)]
    for q in range(4):
        mats_out[q] = mats[q]
    parts = [dot(mats[cc], mats[2 + cc], ((1,), (1,))).reshape(SHARDS, 8, N) for cc in range(2)]
    tri_out[...] = jnp.concatenate(parts, axis=1).astype(BF16)


def heads_sum(x):
    return jnp.sum(x.reshape(HEADS, HEAD_DIM, N), axis=1)


def heads_spread(x):
    return jnp.broadcast_to(x[:, None, :], (HEADS, HEAD_DIM, N)).reshape(C, N)


def attend_kernel(
    tri, z, qh, do, gate, pm, weights, gains, sg_out, that_out, yhat_out, upd_out, kv_out, rstd_out, wide
):
    unpack(tri, wide)
    wo_t = slab(weights, 2)
    wkv_t = jnp.concatenate([slab(weights, 5), slab(weights, 6)], axis=0)
    g_tri, g_pair = twice(gains[1]), twice(gains[2])

    def body(i, carry):
        tri_i = jnp.concatenate([take_rows(wide, i, 16), take_rows(wide, 8 + i, 16)], axis=0)
        that, rstd_t = hat(tri_i)
        upd = dot(wo_t, (that * g_tri).astype(BF16))
        yhat, rstd_y = hat(z[i] + gate[i] * upd)
        kv = dot(wkv_t, (yhat * g_pair).astype(BF16)).astype(BF16)
        kv_f = kv.astype(F32)
        score = heads_sum(qh[i] * kv_f[:C]) * pm[i] + (pm[i] - 1.0) * 1000000000.0
        dot_v = heads_sum(do[i] * kv_f[C:])
        sg_out[i] = jnp.concatenate([score, dot_v], axis=0)
        that_out[i] = that
        yhat_out[i] = yhat
        upd_out[i] = upd
        kv_out[i] = kv
        rstd_out[i] = jnp.concatenate([jnp.broadcast_to(rstd_t, (4, N)), jnp.broadcast_to(rstd_y, (4, N))], axis=0)
        return carry

    each_row(body)


def back_kernel(
    sg, that, yhat, gate, upd, qh, do, kv, rstd, pm, weights, gains,
    dtri_out, dqh_out, dy_out, dgate_out, spread,
):
    t = lax.axis_index("tmpl")
    core = t % 2
    g_tri, g_pair = twice(gains[1]), twice(gains[2])
    wkv_v, wo_v = slab(weights, 0, 2 * C), slab(weights, 3)

    def row(i, n):
        every = [sg[s, i] for s in range(4)]
        own = sg[t, i]
        top = jnp.maximum(jnp.maximum(every[0][:4], every[1][:4]), jnp.maximum(every[2][:4], every[3][:4]))
        expo = [jnp.exp(e[:4] - top) for e in every]
        inv = 1.0 / (expo[0] + expo[1] + expo[2] + expo[3])
        delta = sum(ex * e[4:] for ex, e in zip(expo, every)) * inv
        prob = jnp.exp(own[:4] - top) * inv
        ds = heads_spread(pm[i] * prob * (own[4:] - delta))
        dqh_out[n] = (ds * kv[i].astype(F32)[:C]).astype(BF16)
        d_kv = jnp.concatenate([ds * qh[i], heads_spread(prob) * do[i]], axis=0).astype(BF16)
        rs = rstd[i]
        d_y = hat_back(dot(wkv_v, d_kv) * g_pair, yhat[i], rs[4:5])
        gate_i = gate[i]
        d_upd = d_y * gate_i
        d_gate = (d_upd * upd[i] * (1.0 - gate_i)).astype(BF16)
        dy_out[i] = d_y
        dgate_out[i] = d_gate
        d_tri = hat_back(dot(wo_v, d_upd.astype(BF16)) * g_tri, that[i], rs[0:1])
        put_rows(spread, i, 16, d_tri[:32])
        put_rows(spread, 8 + i, 16, d_tri[32:])

    def body(n, carry):
        row(core * HALF + n, n)
        row((1 - core) * HALF + n, HALF + n)
        return carry

    each_row(body, rows=HALF, unroll=UNROLL // 2)
    pack(spread, dtri_out)


def tri_back_kernel(dtri, mats, dqh, near, out, keep_out):
    keep_out[...] = (dqh[:HALF].astype(F32) + near[HALF:].astype(F32)).astype(BF16)
    wide = dtri[...].astype(F32)
    d = [wide[:, 8 * cc : 8 * cc + 8, :].reshape(N, N).astype(BF16) for cc in range(2)]
    parts = [dot(d[cc], mats[2 + cc]) for cc in range(2)]
    parts += [dot(d[cc], mats[cc], ((0,), (0,))) for cc in range(2)]
    out[...] = jnp.concatenate([p.reshape(SHARDS, 8, N) for p in parts], axis=1).astype(BF16)


def weight_kernel(dlr, ln_b, pm, proj_out, d_out, wide):
    unpack(dlr, wide)

    def body(i, total):
        parts = [take_rows(wide, 8 * q + i, 32) for q in range(4)]
        d = (jnp.concatenate(parts, axis=0) * pm[i]).astype(BF16)
        d_out[i] = d
        return total + dot(ln_b[i], d, ((1,), (1,)))

    proj_out[...] = each_row(body, jnp.zeros((C, 2 * C), F32))


def pair_grad_kernel(d, z, d_y, d_gate, weights, gains, grad_out):
    g = twice(gains[0])
    weight = jnp.concatenate([slab(weights, 1, 2 * C), slab(weights, 4)], axis=1)

    def body(i, carry):
        zhat, rstd = hat(z[i])
        d_ln = dot(weight, jnp.concatenate([d[i], d_gate[i]], axis=0))
        grad_out[i] = d_y[i] + hat_back(d_ln * g, zhat, rstd)
        return carry

    each_row(body)


def query_grad_kernel(own, other, query_h, gain_h, wq_h, out, sems, query, gain, wq_t):
    arrive(copies((query_h, gain_h, wq_h), (query, gain, wq_t), sems))
    core = lax.axis_index("tmpl") % 2
    g = gain[...] * HEAD_DIM ** (-0.5)
    wq_v = wq_t[...]

    def body(i, d_qh):
        x = query[i].astype(F32)
        cent = x - jnp.mean(x, -1, keepdims=True)
        var = jnp.mean(cent * cent, -1, keepdims=True)
        rstd = lax.rsqrt(var + 1e-05)
        xhat = cent * rstd
        dy = dot(d_qh, wq_v, ((0,), (0,))) * g
        out[i] = rstd * (dy - jnp.mean(dy, -1, keepdims=True) - xhat * jnp.mean(dy * xhat, -1, keepdims=True))

    for i in range(HALF):
        body(core * HALF + i, own[i])
        body((1 - core) * HALF + i, other[i])


def fan_kernel(own, far, out):
    total = (own[...] + far[...]).astype(BF16)
    for s in range(SHARDS):
        out[s] = total


def sum_kernel(parts, out):
    total = jnp.sum(parts[...].astype(F32), axis=0)
    out[0] = total[:, :C]
    out[1] = total[:, C:]


def call(kernel, outs, specs, scratch=(), vmem=40, home=VMEM):
    return pl.pallas_call(
        kernel,
        out_shape=[jax.ShapeDtypeStruct(s, d) for s, d in outs],
        in_specs=specs,
        out_specs=[home] * len(outs),
        scratch_shapes=list(scratch),
        compiler_params=pltpu.CompilerParams(vmem_limit_bytes=vmem * 1024 * 1024),
    )


def wide_scratch(rows):
    return pltpu.VMEM((2, rows + rows // SHARDS, 128), F32)


def fetched(*arrays):
    return [pltpu.SemaphoreType.DMA((len(arrays),))] + [pltpu.VMEM(a.shape, a.dtype) for a in arrays]


def stay(*arrays):
    return [pltpu.with_memory_space_constraint(a, pltpu.HBM) for a in arrays]


def swap(x, bit):
    return lax.ppermute(x, "tmpl", [(i, i ^ bit) for i in range(4)])


def after(x, *others):
    return lax.optimization_barrier((x, *others))


def local(
    template_pair, template_mask, residue_index, query_pair, relpos_table, norm_gain, left_weight, right_weight,
    gate_weight, out_weight, tri_gain, pair_gain, kv_weight, query_gain, query_weight, attn_out_weight, cotangent,
):
    pair = jnp.swapaxes(template_pair[0], 1, 2)
    row = lambda x: x.reshape(1, -1)
    every = functools.partial(lax.all_to_all, axis_name="row", split_axis=0, concat_axis=0, tiled=True)
    plane, half = (ROWS, C, N), (ROWS, 2 * C, N)
    sources = (
        left_weight, right_weight, row(norm_gain), relpos_table.T, row(residue_index), residue_index, template_mask,
        template_mask, pair, gate_weight, out_weight, kv_weight, row(tri_gain), row(pair_gain),
    )
    scratch = fetched(*sources)
    for n in (5, 7):
        scratch[1 + n] = pltpu.SMEM(sources[n].shape, sources[n].dtype)
    outs = [((SHARDS, 32, N), BF16), (plane, F32), ((ROWS, 1, N), F32), ((C, 8 * 128), BF16), ((3, C, 128), F32)]
    lr, z, pm, weights, gains = call(
        project_kernel,
        outs,
        [HBM] * 14,
        [pltpu.VMEM((SHARDS, 32, ROWS * C), BF16), pltpu.VMEM((ROWS * C, N), BF16)] + scratch,
    )(*stay(*sources))
    lr_all = every(lr)
    prepared = call(prepare_kernel, [(plane, BF16)] + [(plane, F32)] * 3, [VMEM] * 8)(
        z, weights, gains, query_pair, cotangent, row(query_gain), query_weight.T, attn_out_weight
    )
    lr_all, ln_b, qh, do, gate = after(lr_all, *prepared)
    tri, mats = call(tri_kernel, [((SHARDS, 16, N), BF16), ((4, N, N), BF16)], [VMEM])(lr_all)
    tri = every(tri)
    sg, that, yhat, upd, kv, rstd = call(
        attend_kernel,
        [((ROWS, 8, N), F32)] + [(plane, F32)] * 3 + [(half, BF16), ((ROWS, 8, N), F32)],
        [VMEM] * 8,
        [wide_scratch(SHARDS * 16)],
    )(tri, z, qh, do, gate, pm, weights, gains)
    sg = lax.all_gather(sg, "tmpl")
    dtri, dqh, d_y, d_gate = call(
        back_kernel,
        [((SHARDS, 16, N), BF16), (plane, BF16), (plane, F32), (plane, BF16)],
        [VMEM] * 12,
        [wide_scratch(SHARDS * 16)],
    )(sg, that, yhat, gate, upd, qh, do, kv, rstd, pm, weights, gains)
    dlr, keep = call(tri_back_kernel, [((SHARDS, 32, N), BF16), ((HALF, C, N), BF16)], [VMEM] * 4)(
        every(dtri), mats, dqh, swap(dqh, 1)
    )
    dlr, keep = after(every(dlr), keep)
    proj, d = call(
        weight_kernel, [((C, 2 * C), F32), (half, BF16)], [VMEM] * 3, [wide_scratch(SHARDS * 32)]
    )(dlr, ln_b, pm)
    near = swap(proj, 1)
    (grad,) = call(pair_grad_kernel, [(plane, F32)], [VMEM] * 6)(d, z, d_y, d_gate, weights, gains)
    proj = proj + near
    (fan,) = call(fan_kernel, [((SHARDS, C, 2 * C), BF16)], [VMEM] * 2)(proj, swap(proj, 2))
    fan, grad, own = after(fan, grad, keep + swap(keep, 2))
    parts = every(fan)
    sources = (query_pair, row(query_gain), query_weight.T)
    (query_grad,) = call(
        query_grad_kernel, [((ROWS, N, 2 * C), F32)], [VMEM] * 2 + [HBM] * 3, fetched(*sources)
    )(own, swap(own, 1), *sources)
    parts, query_grad = after(parts, query_grad)
    (proj,) = call(sum_kernel, [((2, C, C), F32)], [VMEM])(parts)
    return jnp.swapaxes(grad, 1, 2)[None], query_grad, proj


def solution(mesh):
    in_specs = (
        P("tmpl", "row", None, None),
        P(),
        P(),
        P("row", None, None),
        *([P()] * 12),
        P("row", None, None),
    )
    out_specs = (P("tmpl", "row", None, None), P("row", None, None), P())
    return jax.shard_map(local, mesh=mesh, in_specs=in_specs, out_specs=out_specs, check_vma=False)
```

```python
import functools

import jax
import jax.numpy as jnp
from jax import lax
from jax.experimental import pallas as pl
from jax.experimental.pallas import tpu as pltpu
from jax.sharding import PartitionSpec as P

F32 = jnp.float32
BF16 = jnp.bfloat16
HEADS = 4
HEAD_DIM = 16
C = 64
ROWS = 8
N = 256
SHARDS = 32
UNROLL = 8
HALF = ROWS // 2
PIECES = 4
HBM = pl.BlockSpec(memory_space=pltpu.HBM)
VMEM = pl.BlockSpec(memory_space=pltpu.VMEM)


def dot(a, b, contract=((1,), (0,))):
    return lax.dot_general(a, b, (contract, ((), ())), preferred_element_type=F32)


def fine_dot(a, x, contract=((1,), (0,))):
    high = x.astype(BF16)
    low = (x - high.astype(F32)).astype(BF16)
    return dot(a, high, contract) + dot(a, low, contract)


def flip(x):
    return x.astype(F32).T


def column(row):
    return jnp.broadcast_to(row, (128, row.shape[1])).T


def twice(x):
    return jnp.concatenate([x, x], axis=1)


def slab(weights, n, width=C):
    return weights[:, 128 * n : 128 * n + width]


def hat(x):
    mean = jnp.mean(x, 0, keepdims=True)
    cent = x - mean
    var = jnp.mean(cent * cent, 0, keepdims=True)
    rstd = lax.rsqrt(var + 1e-05)
    return cent * rstd, rstd


def hat_back(dy, xhat, rstd):
    return rstd * (dy - jnp.mean(dy, 0, keepdims=True) - xhat * jnp.mean(dy * xhat, 0, keepdims=True))


def owner_rows(left, right):
    rows = jnp.concatenate([left, right], axis=0)
    rows = jnp.concatenate([rows, rows], axis=1)
    sub = lax.broadcasted_iota(jnp.int32, (8, 128), 0)
    lane = lax.broadcasted_iota(jnp.int32, (8, 128), 1) // C
    tiles = []
    for pair in range(ROWS // 2):
        mine = (sub == 2 * pair + lane)[None, None]
        spread = jnp.broadcast_to(rows.reshape(4, SHARDS, 1, 128), (4, SHARDS, 8, 128))
        tiles.append(jnp.where(mine, spread, 0.0))
    return tiles


def put_rows(spread, first, step, x):
    for half in range(2):
        spread[half, pl.ds(first, x.shape[0], stride=step), :] = x[:, 128 * half : 128 * half + 128]


def pack(spread, out):
    for half in range(2):
        rows = spread[half, : out.shape[0] * out.shape[1]]
        out[:, :, 128 * half : 128 * half + 128] = rows.reshape(out.shape[0], out.shape[1], 128).astype(BF16)


def take_rows(wide, first, step):
    return jnp.concatenate([wide[half, pl.ds(first, SHARDS, stride=step), :] for half in range(2)], axis=1)


def unpack(x, wide):
    rows = x.shape[0] * x.shape[1]
    for half in range(2):
        wide[half, :rows] = x[:, :, 128 * half : 128 * half + 128].astype(F32).reshape(rows, 128)


def place(rows_ref):
    t = lax.axis_index("tmpl")
    start = lax.axis_index("row") * ROWS
    mask_row = rows_ref[pl.ds(t, 1), :].astype(F32)
    return t, start, mask_row


def each_row(body, carry=0, rows=ROWS, unroll=UNROLL):
    def step(s, carry):
        for u in range(unroll):
            carry = body(s * unroll + u, carry)
        return carry

    if unroll == rows:
        return step(0, carry)
    return lax.fori_loop(0, rows // unroll, step, carry)


def copies(sources, places, sems, first=0):
    started = [pltpu.make_async_copy(src, dst, sems.at[first + n]) for n, (src, dst) in enumerate(zip(sources, places))]
    for copy in started:
        copy.start()
    return started


def arrive(started):
    for copy in started:
        copy.wait()


def relative(res_s, residues, table, at):
    bins = lax.broadcasted_iota(jnp.int32, (128, N), 0)
    offset = jnp.clip(res_s[at] - residues, -64, 63) + 64
    return dot(table, jnp.where(bins == offset, 1.0, 0.0).astype(BF16))


def project_kernel(*refs):
    sources, outs, places = refs[:19], refs[19:28], refs[30:]
    lhs, sems = refs[28:30]
    lr, z, pm, weights, gains, normed, qh_out, do_out, gate_out = outs
    arriving = copies(sources, places, sems)
    wl, wr, norm_gain, table_t, res, res_s, mask, mask_s, pair, wg, wo, wkv, tri_gain, pair_gain = places[:14]
    query, cot, q_gain, wq_t, wao = places[14:]
    arrive(arriving[:2])
    for pair_of, tile in enumerate(owner_rows(flip(wl[...]), flip(wr[...]))):
        for side in range(2):
            both = jnp.concatenate([tile[2 * side], tile[2 * side + 1]], axis=1)
            lhs[:, 16 * side : 16 * side + 16, 128 * pair_of : 128 * pair_of + 128] = both.astype(BF16)
    arrive(arriving[2:9])
    t, start, mask_row = place(mask)
    table, residues, gain = table_t[...], res[...], column(norm_gain[...])
    g = twice(gain)

    def body(i, carry):
        z_i = pair[i].astype(F32) + relative(res_s, residues, table, start + i)
        z[i] = z_i
        pm_i = mask_row * mask_s[t, start + i].astype(F32)
        pm[i] = pm_i
        normed[i] = (hat(z_i)[0] * g).astype(BF16)
        return carry

    each_row(body)
    arrive(arriving[9:])
    blank = jnp.zeros((C, C), BF16)
    wkv_t = flip(wkv[...]).astype(BF16)
    parts = [wkv[...], wl[...], wr[...], flip(wo[...]).astype(BF16), blank, wo[...], blank, wg[...], blank]
    parts += [wkv_t[:C], blank, wkv_t[C:], blank, flip(wg[...]).astype(BF16), blank]
    weights[...] = jnp.concatenate(parts, axis=1)
    gains[0] = gain
    gains[1] = column(tri_gain[...])
    gains[2] = column(pair_gain[...])
    some = SHARDS // PIECES
    for p in range(PIECES):
        owners = slice(p * some, (p + 1) * some)
        both = dot(lhs[owners].reshape(some * 32, ROWS * C), normed[...].reshape(ROWS * C, N)).reshape(some * 4, ROWS, N)
        lr[owners] = (both * pm[...].reshape(1, ROWS, N)).reshape(some, 32, N).astype(BF16)

    wg_t = flip(wg[...]).astype(BF16)
    wq_v, wao_v, g_query = wq_t[...], wao[...], q_gain[...]

    def heads(i, carry):
        x = query[i].astype(F32)
        cent = x - jnp.mean(x, -1, keepdims=True)
        var = jnp.mean(cent * cent, -1, keepdims=True)
        qn = cent * lax.rsqrt(var + 1e-05) * g_query
        qh_out[i] = fine_dot(wq_v, qn, ((1,), (1,))) * HEAD_DIM ** (-0.5)
        do_out[i] = dot(wao_v, cot[i], ((1,), (1,)))
        gate_out[i] = jax.nn.sigmoid(fine_dot(wg_t, hat(z[i])[0] * g))
        return carry

    each_row(heads)


def tri_kernel(lr, tri_out, mats_out):
    wide = lr[...].astype(F32)
    mats = [wide[:, 8 * q : 8 * q + 8, :].reshape(N, N).astype(BF16) for q in range(4)]
    for q in range(4):
        mats_out[q] = mats[q]
    parts = [dot(mats[cc], mats[2 + cc], ((1,), (1,))).reshape(SHARDS, 8, N) for cc in range(2)]
    tri_out[...] = jnp.concatenate(parts, axis=1).astype(BF16)


def heads_sum(x):
    return jnp.sum(x.reshape(HEADS, HEAD_DIM, N), axis=1)


def heads_spread(x):
    return jnp.broadcast_to(x[:, None, :], (HEADS, HEAD_DIM, N)).reshape(C, N)


def attend_kernel(
    tri, z, qh, do, gate, pm, weights, gains, sg_out, that_out, yhat_out, upd_out, kv_out, rstd_out, wide
):
    unpack(tri, wide)
    wo_t = slab(weights, 2)
    wkv_t = jnp.concatenate([slab(weights, 5), slab(weights, 6)], axis=0)
    g_tri, g_pair = twice(gains[1]), twice(gains[2])

    def body(i, carry):
        tri_i = jnp.concatenate([take_rows(wide, i, 16), take_rows(wide, 8 + i, 16)], axis=0)
        that, rstd_t = hat(tri_i)
        upd = fine_dot(wo_t, that * g_tri)
        yhat, rstd_y = hat(z[i] + gate[i] * upd)
        kv = fine_dot(wkv_t, yhat * g_pair).astype(BF16)
        kv_f = kv.astype(F32)
        score = heads_sum(qh[i] * kv_f[:C]) * pm[i] + (pm[i] - 1.0) * 1000000000.0
        dot_v = heads_sum(do[i] * kv_f[C:])
        sg_out[i] = jnp.concatenate([score, dot_v], axis=0)
        that_out[i] = that
        yhat_out[i] = yhat
        upd_out[i] = upd
        kv_out[i] = kv
        rstd_out[i] = jnp.concatenate([jnp.broadcast_to(rstd_t, (4, N)), jnp.broadcast_to(rstd_y, (4, N))], axis=0)
        return carry

    each_row(body)


def back_kernel(
    sg, that, yhat, gate, upd, qh, do, kv, rstd, pm, weights, gains,
    dtri_out, dqh_out, dy_out, dgate_out, spread,
):
    t = lax.axis_index("tmpl")
    core = t % 2
    g_tri, g_pair = twice(gains[1]), twice(gains[2])
    wkv_v, wo_v = slab(weights, 0, 2 * C), slab(weights, 3)

    def row(i, n):
        every = [sg[s, i] for s in range(4)]
        own = sg[t, i]
        top = jnp.maximum(jnp.maximum(every[0][:4], every[1][:4]), jnp.maximum(every[2][:4], every[3][:4]))
        expo = [jnp.exp(e[:4] - top) for e in every]
        inv = 1.0 / (expo[0] + expo[1] + expo[2] + expo[3])
        delta = sum(ex * e[4:] for ex, e in zip(expo, every)) * inv
        prob = jnp.exp(own[:4] - top) * inv
        ds = heads_spread(pm[i] * prob * (own[4:] - delta))
        dqh_out[n] = ds * kv[i].astype(F32)[:C]
        d_kv = jnp.concatenate([ds * qh[i], heads_spread(prob) * do[i]], axis=0).astype(BF16)
        rs = rstd[i]
        d_y = hat_back(dot(wkv_v, d_kv) * g_pair, yhat[i], rs[4:5])
        gate_i = gate[i]
        d_upd = d_y * gate_i
        d_gate = (d_upd * upd[i] * (1.0 - gate_i)).astype(BF16)
        dy_out[i] = d_y
        dgate_out[i] = d_gate
        d_tri = hat_back(dot(wo_v, d_upd.astype(BF16)) * g_tri, that[i], rs[0:1])
        put_rows(spread, i, 16, d_tri[:32])
        put_rows(spread, 8 + i, 16, d_tri[32:])

    def body(n, carry):
        row(core * HALF + n, n)
        row((1 - core) * HALF + n, HALF + n)
        return carry

    each_row(body, rows=HALF, unroll=UNROLL // 2)
    pack(spread, dtri_out)


def tri_back_kernel(dtri, mats, dqh, near, out, keep_out):
    keep_out[...] = dqh[:HALF] + near[HALF:]
    wide = dtri[...].astype(F32)
    d = [wide[:, 8 * cc : 8 * cc + 8, :].reshape(N, N).astype(BF16) for cc in range(2)]
    parts = [dot(d[cc], mats[2 + cc]) for cc in range(2)]
    parts += [dot(d[cc], mats[cc], ((0,), (0,))) for cc in range(2)]
    out[...] = jnp.concatenate([p.reshape(SHARDS, 8, N) for p in parts], axis=1).astype(BF16)


def weight_kernel(dlr, ln_b, pm, proj_out, d_out, wide):
    unpack(dlr, wide)

    def body(i, total):
        parts = [take_rows(wide, 8 * q + i, 32) for q in range(4)]
        d = (jnp.concatenate(parts, axis=0) * pm[i]).astype(BF16)
        d_out[i] = d
        return total + dot(ln_b[i], d, ((1,), (1,)))

    proj_out[...] = each_row(body, jnp.zeros((C, 2 * C), F32))


def pair_grad_kernel(d, z, d_y, d_gate, weights, gains, grad_out):
    g = twice(gains[0])
    weight = jnp.concatenate([slab(weights, 1, 2 * C), slab(weights, 4)], axis=1)

    def body(i, carry):
        zhat, rstd = hat(z[i])
        d_ln = dot(weight, jnp.concatenate([d[i], d_gate[i]], axis=0))
        grad_out[i] = d_y[i] + hat_back(d_ln * g, zhat, rstd)
        return carry

    each_row(body)


def query_grad_kernel(own, other, query_h, gain_h, wq_h, out, sems, query, gain, wq_t):
    arrive(copies((query_h, gain_h, wq_h), (query, gain, wq_t), sems))
    core = lax.axis_index("tmpl") % 2
    g = gain[...] * HEAD_DIM ** (-0.5)
    wq_v = wq_t[...]

    def body(i, d_qh):
        x = query[i].astype(F32)
        cent = x - jnp.mean(x, -1, keepdims=True)
        var = jnp.mean(cent * cent, -1, keepdims=True)
        rstd = lax.rsqrt(var + 1e-05)
        xhat = cent * rstd
        dy = dot(d_qh, wq_v, ((0,), (0,))) * g
        out[i] = rstd * (dy - jnp.mean(dy, -1, keepdims=True) - xhat * jnp.mean(dy * xhat, -1, keepdims=True))

    for i in range(HALF):
        body(core * HALF + i, own[i])
        body((1 - core) * HALF + i, other[i])


def fan_kernel(own, far, out):
    total = (own[...] + far[...]).astype(BF16)
    for s in range(SHARDS):
        out[s] = total


def sum_kernel(parts, out):
    total = jnp.sum(parts[...].astype(F32), axis=0)
    out[0] = total[:, :C]
    out[1] = total[:, C:]


def call(kernel, outs, specs, scratch=(), vmem=40, home=VMEM):
    return pl.pallas_call(
        kernel,
        out_shape=[jax.ShapeDtypeStruct(s, d) for s, d in outs],
        in_specs=specs,
        out_specs=[home] * len(outs),
        scratch_shapes=list(scratch),
        compiler_params=pltpu.CompilerParams(vmem_limit_bytes=vmem * 1024 * 1024),
    )


def wide_scratch(rows):
    return pltpu.VMEM((2, rows + rows // SHARDS, 128), F32)


def fetched(*arrays):
    return [pltpu.SemaphoreType.DMA((len(arrays),))] + [pltpu.VMEM(a.shape, a.dtype) for a in arrays]


def stay(*arrays):
    return [pltpu.with_memory_space_constraint(a, pltpu.HBM) for a in arrays]


def swap(x, bit):
    return lax.ppermute(x, "tmpl", [(i, i ^ bit) for i in range(4)])


def after(x, *others):
    return lax.optimization_barrier((x, *others))


def local(
    template_pair, template_mask, residue_index, query_pair, relpos_table, norm_gain, left_weight, right_weight,
    gate_weight, out_weight, tri_gain, pair_gain, kv_weight, query_gain, query_weight, attn_out_weight, cotangent,
):
    pair = jnp.swapaxes(template_pair[0], 1, 2)
    row = lambda x: x.reshape(1, -1)
    every = functools.partial(lax.all_to_all, axis_name="row", split_axis=0, concat_axis=0, tiled=True)
    plane, half = (ROWS, C, N), (ROWS, 2 * C, N)
    sources = (
        left_weight, right_weight, row(norm_gain), relpos_table.T, row(residue_index), residue_index, template_mask,
        template_mask, pair, gate_weight, out_weight, kv_weight, row(tri_gain), row(pair_gain),
        query_pair, cotangent, row(query_gain), query_weight.T, attn_out_weight,
    )
    scratch = fetched(*sources)
    for n in (5, 7):
        scratch[1 + n] = pltpu.SMEM(sources[n].shape, sources[n].dtype)
    outs = [((SHARDS, 32, N), BF16), (plane, F32), ((ROWS, 1, N), F32), ((C, 8 * 128), BF16), ((3, C, 128), F32)]
    outs += [(plane, BF16)] + [(plane, F32)] * 3
    lr, z, pm, weights, gains, ln_b, qh, do, gate = call(
        project_kernel, outs, [HBM] * 19, [pltpu.VMEM((SHARDS, 32, ROWS * C), BF16)] + scratch
    )(*stay(*sources))
    tri, mats = call(tri_kernel, [((SHARDS, 16, N), BF16), ((4, N, N), BF16)], [VMEM])(every(lr))
    tri = every(tri)
    sg, that, yhat, upd, kv, rstd = call(
        attend_kernel,
        [((ROWS, 8, N), F32)] + [(plane, F32)] * 3 + [(half, BF16), ((ROWS, 8, N), F32)],
        [VMEM] * 8,
        [wide_scratch(SHARDS * 16)],
    )(tri, z, qh, do, gate, pm, weights, gains)
    sg = lax.all_gather(sg, "tmpl")
    dtri, dqh, d_y, d_gate = call(
        back_kernel,
        [((SHARDS, 16, N), BF16), (plane, F32), (plane, F32), (plane, BF16)],
        [VMEM] * 12,
        [wide_scratch(SHARDS * 16)],
    )(sg, that, yhat, gate, upd, qh, do, kv, rstd, pm, weights, gains)
    dlr, keep = call(tri_back_kernel, [((SHARDS, 32, N), BF16), ((HALF, C, N), F32)], [VMEM] * 4)(
        every(dtri), mats, dqh, swap(dqh, 1)
    )
    dlr, keep = after(every(dlr), keep)
    proj, d = call(
        weight_kernel, [((C, 2 * C), F32), (half, BF16)], [VMEM] * 3, [wide_scratch(SHARDS * 32)]
    )(dlr, ln_b, pm)
    near = swap(proj, 1)
    (grad,) = call(pair_grad_kernel, [(plane, F32)], [VMEM] * 6)(d, z, d_y, d_gate, weights, gains)
    proj = proj + near
    (fan,) = call(fan_kernel, [((SHARDS, C, 2 * C), BF16)], [VMEM] * 2)(proj, swap(proj, 2))
    fan, grad, own = after(fan, grad, (keep + swap(keep, 2)).astype(BF16))
    parts = every(fan)
    sources = (query_pair, row(query_gain), query_weight.T)
    (query_grad,) = call(
        query_grad_kernel, [((ROWS, N, 2 * C), F32)], [VMEM] * 2 + [HBM] * 3, fetched(*sources)
    )(own, swap(own, 1), *sources)
    parts, query_grad = after(parts, query_grad)
    (proj,) = call(sum_kernel, [((2, C, C), F32)], [VMEM])(parts)
    return jnp.swapaxes(grad, 1, 2)[None], query_grad, proj


def solution(mesh):
    in_specs = (
        P("tmpl", "row", None, None),
        P(),
        P(),
        P("row", None, None),
        *([P()] * 12),
        P("row", None, None),
    )
    out_specs = (P("tmpl", "row", None, None), P("row", None, None), P())
    return jax.shard_map(local, mesh=mesh, in_specs=in_specs, out_specs=out_specs, check_vma=False)
```

```python
import functools

import jax
import jax.numpy as jnp
from jax import lax
from jax.experimental import pallas as pl
from jax.experimental.pallas import tpu as pltpu
from jax.sharding import PartitionSpec as P

F32 = jnp.float32
BF16 = jnp.bfloat16
HEADS = 4
HEAD_DIM = 16
C = 64
ROWS = 8
N = 256
SHARDS = 32
UNROLL = 8
HALF = ROWS // 2
PIECES = 4
HBM = pl.BlockSpec(memory_space=pltpu.HBM)
VMEM = pl.BlockSpec(memory_space=pltpu.VMEM)


def dot(a, b, contract=((1,), (0,))):
    return lax.dot_general(a, b, (contract, ((), ())), preferred_element_type=F32)


def fine_dot(a, x, contract=((1,), (0,))):
    high = x.astype(BF16)
    low = (x - high.astype(F32)).astype(BF16)
    return dot(a, high, contract) + dot(a, low, contract)


def flip(x):
    return x.astype(F32).T


def column(row):
    return jnp.broadcast_to(row, (128, row.shape[1])).T


def twice(x):
    return jnp.concatenate([x, x], axis=1)


def slab(weights, n, width=C):
    return weights[:, 128 * n : 128 * n + width]


def hat(x):
    mean = jnp.mean(x, 0, keepdims=True)
    cent = x - mean
    var = jnp.mean(cent * cent, 0, keepdims=True)
    rstd = lax.rsqrt(var + 1e-05)
    return cent * rstd, rstd


def hat_back(dy, xhat, rstd):
    return rstd * (dy - jnp.mean(dy, 0, keepdims=True) - xhat * jnp.mean(dy * xhat, 0, keepdims=True))


def owner_rows(left, right):
    rows = jnp.concatenate([left, right], axis=0)
    rows = jnp.concatenate([rows, rows], axis=1)
    sub = lax.broadcasted_iota(jnp.int32, (8, 128), 0)
    lane = lax.broadcasted_iota(jnp.int32, (8, 128), 1) // C
    tiles = []
    for pair in range(ROWS // 2):
        mine = (sub == 2 * pair + lane)[None, None]
        spread = jnp.broadcast_to(rows.reshape(4, SHARDS, 1, 128), (4, SHARDS, 8, 128))
        tiles.append(jnp.where(mine, spread, 0.0))
    return tiles


def put_rows(spread, first, step, x):
    for half in range(2):
        spread[half, pl.ds(first, x.shape[0], stride=step), :] = x[:, 128 * half : 128 * half + 128]


def pack(spread, out):
    for half in range(2):
        rows = spread[half, : out.shape[0] * out.shape[1]]
        out[:, :, 128 * half : 128 * half + 128] = rows.reshape(out.shape[0], out.shape[1], 128).astype(BF16)


def take_rows(wide, first, step):
    return jnp.concatenate([wide[half, pl.ds(first, SHARDS, stride=step), :] for half in range(2)], axis=1)


def unpack(x, wide):
    rows = x.shape[0] * x.shape[1]
    for half in range(2):
        wide[half, :rows] = x[:, :, 128 * half : 128 * half + 128].astype(F32).reshape(rows, 128)


def place(rows_ref):
    t = lax.axis_index("tmpl")
    start = lax.axis_index("row") * ROWS
    mask_row = rows_ref[pl.ds(t, 1), :].astype(F32)
    return t, start, mask_row


def each_row(body, carry=0, rows=ROWS, unroll=UNROLL):
    def step(s, carry):
        for u in range(unroll):
            carry = body(s * unroll + u, carry)
        return carry

    if unroll == rows:
        return step(0, carry)
    return lax.fori_loop(0, rows // unroll, step, carry)


def copies(sources, places, sems, first=0):
    started = [pltpu.make_async_copy(src, dst, sems.at[first + n]) for n, (src, dst) in enumerate(zip(sources, places))]
    for copy in started:
        copy.start()
    return started


def arrive(started):
    for copy in started:
        copy.wait()


def relative(res_s, residues, table, at):
    bins = lax.broadcasted_iota(jnp.int32, (128, N), 0)
    offset = jnp.clip(res_s[at] - residues, -64, 63) + 64
    return dot(table, jnp.where(bins == offset, 1.0, 0.0).astype(BF16))


def project_kernel(*refs):
    sources, outs, places = refs[:19], refs[19:28], refs[30:]
    lhs, sems = refs[28:30]
    lr, z, pm, weights, gains, normed, qh_out, do_out, gate_out = outs
    arriving = copies(sources, places, sems)
    wl, wr, norm_gain, table_t, res, res_s, mask, mask_s, pair, wg, wo, wkv, tri_gain, pair_gain = places[:14]
    query, cot, q_gain, wq_t, wao = places[14:]
    arrive(arriving[:2])
    for pair_of, tile in enumerate(owner_rows(flip(wl[...]), flip(wr[...]))):
        for side in range(2):
            both = jnp.concatenate([tile[2 * side], tile[2 * side + 1]], axis=1)
            lhs[:, 16 * side : 16 * side + 16, 128 * pair_of : 128 * pair_of + 128] = both.astype(BF16)
    arrive(arriving[2:9])
    t, start, mask_row = place(mask)
    table, residues, gain = table_t[...], res[...], column(norm_gain[...])
    g = twice(gain)

    def body(i, carry):
        z_i = pair[i].astype(F32) + relative(res_s, residues, table, start + i)
        z[i] = z_i
        pm_i = mask_row * mask_s[t, start + i].astype(F32)
        pm[i] = pm_i
        normed[i] = (hat(z_i)[0] * g).astype(BF16)
        return carry

    each_row(body)
    arrive(arriving[9:])
    blank = jnp.zeros((C, C), BF16)
    wkv_t = flip(wkv[...]).astype(BF16)
    parts = [wkv[...], wl[...], wr[...], flip(wo[...]).astype(BF16), blank, wo[...], blank, wg[...], blank]
    parts += [wkv_t[:C], blank, wkv_t[C:], blank, flip(wg[...]).astype(BF16), blank]
    weights[...] = jnp.concatenate(parts, axis=1)
    gains[0] = gain
    gains[1] = column(tri_gain[...])
    gains[2] = column(pair_gain[...])
    some = SHARDS // PIECES
    for p in range(PIECES):
        owners = slice(p * some, (p + 1) * some)
        both = dot(lhs[owners].reshape(some * 32, ROWS * C), normed[...].reshape(ROWS * C, N)).reshape(some * 4, ROWS, N)
        lr[owners] = (both * pm[...].reshape(1, ROWS, N)).reshape(some, 32, N).astype(BF16)

    wg_t = flip(wg[...]).astype(BF16)
    wq_v, wao_v, g_query = wq_t[...], wao[...], q_gain[...]

    def heads(i, carry):
        x = query[i].astype(F32)
        cent = x - jnp.mean(x, -1, keepdims=True)
        var = jnp.mean(cent * cent, -1, keepdims=True)
        qn = cent * lax.rsqrt(var + 1e-05) * g_query
        qh_out[i] = fine_dot(wq_v, qn, ((1,), (1,))) * HEAD_DIM ** (-0.5)
        do_out[i] = dot(wao_v, cot[i], ((1,), (1,)))
        gate_out[i] = jax.nn.sigmoid(fine_dot(wg_t, hat(z[i])[0] * g))
        return carry

    each_row(heads)


def tri_kernel(lr, tri_out, mats_out):
    wide = lr[...].astype(F32)
    mats = [wide[:, 8 * q : 8 * q + 8, :].reshape(N, N).astype(BF16) for q in range(4)]
    for q in range(4):
        mats_out[q] = mats[q]
    parts = [dot(mats[cc], mats[2 + cc], ((1,), (1,))).reshape(SHARDS, 8, N) for cc in range(2)]
    tri_out[...] = jnp.concatenate(parts, axis=1).astype(BF16)


def heads_sum(x):
    return jnp.sum(x.reshape(HEADS, HEAD_DIM, N), axis=1)


def heads_spread(x):
    return jnp.broadcast_to(x[:, None, :], (HEADS, HEAD_DIM, N)).reshape(C, N)


def attend_kernel(
    tri, z, qh, do, gate, pm, weights, gains, sg_out, that_out, yhat_out, upd_out, kv_out, rstd_out, wide
):
    unpack(tri, wide)
    wo_t = slab(weights, 2)
    wkv_t = jnp.concatenate([slab(weights, 5), slab(weights, 6)], axis=0)
    g_tri, g_pair = twice(gains[1]), twice(gains[2])

    def body(i, carry):
        tri_i = jnp.concatenate([take_rows(wide, i, 16), take_rows(wide, 8 + i, 16)], axis=0)
        that, rstd_t = hat(tri_i)
        upd = fine_dot(wo_t, that * g_tri)
        yhat, rstd_y = hat(z[i] + gate[i] * upd)
        kv = fine_dot(wkv_t, yhat * g_pair).astype(BF16)
        kv_f = kv.astype(F32)
        score = heads_sum(qh[i] * kv_f[:C]) * pm[i] + (pm[i] - 1.0) * 1000000000.0
        dot_v = heads_sum(do[i] * kv_f[C:])
        sg_out[i] = jnp.concatenate([score, dot_v], axis=0)
        that_out[i] = that
        yhat_out[i] = yhat
        upd_out[i] = upd
        kv_out[i] = kv
        rstd_out[i] = jnp.concatenate([jnp.broadcast_to(rstd_t, (4, N)), jnp.broadcast_to(rstd_y, (4, N))], axis=0)
        return carry

    each_row(body)


def back_kernel(
    sg, that, yhat, gate, upd, qh, do, kv, rstd, pm, weights, gains,
    dtri_out, dqh_out, dy_out, dgate_out, spread,
):
    t = lax.axis_index("tmpl")
    core = t % 2
    g_tri, g_pair = twice(gains[1]), twice(gains[2])
    wkv_v, wo_v = slab(weights, 0, 2 * C), slab(weights, 3)

    def row(i, n):
        every = [sg[s, i] for s in range(4)]
        own = sg[t, i]
        top = jnp.maximum(jnp.maximum(every[0][:4], every[1][:4]), jnp.maximum(every[2][:4], every[3][:4]))
        expo = [jnp.exp(e[:4] - top) for e in every]
        inv = 1.0 / (expo[0] + expo[1] + expo[2] + expo[3])
        delta = sum(ex * e[4:] for ex, e in zip(expo, every)) * inv
        prob = jnp.exp(own[:4] - top) * inv
        ds = heads_spread(pm[i] * prob * (own[4:] - delta))
        dqh_out[n] = ds * kv[i].astype(F32)[:C]
        d_kv = jnp.concatenate([ds * qh[i], heads_spread(prob) * do[i]], axis=0).astype(BF16)
        rs = rstd[i]
        d_y = hat_back(dot(wkv_v, d_kv) * g_pair, yhat[i], rs[4:5])
        gate_i = gate[i]
        d_upd = d_y * gate_i
        d_gate = (d_upd * upd[i] * (1.0 - gate_i)).astype(BF16)
        dy_out[i] = d_y
        dgate_out[i] = d_gate
        d_tri = hat_back(dot(wo_v, d_upd.astype(BF16)) * g_tri, that[i], rs[0:1])
        put_rows(spread, i, 16, d_tri[:32])
        put_rows(spread, 8 + i, 16, d_tri[32:])

    def body(n, carry):
        row(core * HALF + n, n)
        row((1 - core) * HALF + n, HALF + n)
        return carry

    each_row(body, rows=HALF, unroll=UNROLL // 2)
    pack(spread, dtri_out)


def tri_back_kernel(dtri, mats, dqh, near, out, keep_out):
    keep_out[...] = (dqh[:HALF] + near[HALF:]).astype(BF16)
    wide = dtri[...].astype(F32)
    d = [wide[:, 8 * cc : 8 * cc + 8, :].reshape(N, N).astype(BF16) for cc in range(2)]
    parts = [dot(d[cc], mats[2 + cc]) for cc in range(2)]
    parts += [dot(d[cc], mats[cc], ((0,), (0,))) for cc in range(2)]
    out[...] = jnp.concatenate([p.reshape(SHARDS, 8, N) for p in parts], axis=1).astype(BF16)


def weight_kernel(dlr, ln_b, pm, proj_out, d_out, wide):
    unpack(dlr, wide)

    def body(i, total):
        parts = [take_rows(wide, 8 * q + i, 32) for q in range(4)]
        d = (jnp.concatenate(parts, axis=0) * pm[i]).astype(BF16)
        d_out[i] = d
        return total + dot(ln_b[i], d, ((1,), (1,)))

    proj_out[...] = each_row(body, jnp.zeros((C, 2 * C), F32))


def pair_grad_kernel(d, z, d_y, d_gate, weights, gains, grad_out):
    g = twice(gains[0])
    weight = jnp.concatenate([slab(weights, 1, 2 * C), slab(weights, 4)], axis=1)

    def body(i, carry):
        zhat, rstd = hat(z[i])
        d_ln = dot(weight, jnp.concatenate([d[i], d_gate[i]], axis=0))
        grad_out[i] = d_y[i] + hat_back(d_ln * g, zhat, rstd)
        return carry

    each_row(body)


def query_grad_kernel(own, other, query_h, gain_h, wq_h, out, sems, query, gain, wq_t):
    arrive(copies((query_h, gain_h, wq_h), (query, gain, wq_t), sems))
    core = lax.axis_index("tmpl") % 2
    g = gain[...] * HEAD_DIM ** (-0.5)
    wq_v = wq_t[...]

    def body(i, d_qh):
        x = query[i].astype(F32)
        cent = x - jnp.mean(x, -1, keepdims=True)
        var = jnp.mean(cent * cent, -1, keepdims=True)
        rstd = lax.rsqrt(var + 1e-05)
        xhat = cent * rstd
        dy = dot(d_qh, wq_v, ((0,), (0,))) * g
        out[i] = rstd * (dy - jnp.mean(dy, -1, keepdims=True) - xhat * jnp.mean(dy * xhat, -1, keepdims=True))

    for i in range(HALF):
        body(core * HALF + i, own[i])
        body((1 - core) * HALF + i, other[i])


def fan_kernel(own, far, out):
    total = (own[...] + far[...]).astype(BF16)
    for s in range(SHARDS):
        out[s] = total


def sum_kernel(parts, out):
    total = jnp.sum(parts[...].astype(F32), axis=0)
    out[0] = total[:, :C]
    out[1] = total[:, C:]


def call(kernel, outs, specs, scratch=(), vmem=40, home=VMEM):
    return pl.pallas_call(
        kernel,
        out_shape=[jax.ShapeDtypeStruct(s, d) for s, d in outs],
        in_specs=specs,
        out_specs=[home] * len(outs),
        scratch_shapes=list(scratch),
        compiler_params=pltpu.CompilerParams(vmem_limit_bytes=vmem * 1024 * 1024),
    )


def wide_scratch(rows):
    return pltpu.VMEM((2, rows + rows // SHARDS, 128), F32)


def fetched(*arrays):
    return [pltpu.SemaphoreType.DMA((len(arrays),))] + [pltpu.VMEM(a.shape, a.dtype) for a in arrays]


def stay(*arrays):
    return [pltpu.with_memory_space_constraint(a, pltpu.HBM) for a in arrays]


def swap(x, bit):
    return lax.ppermute(x, "tmpl", [(i, i ^ bit) for i in range(4)])


def after(x, *others):
    return lax.optimization_barrier((x, *others))


def local(
    template_pair, template_mask, residue_index, query_pair, relpos_table, norm_gain, left_weight, right_weight,
    gate_weight, out_weight, tri_gain, pair_gain, kv_weight, query_gain, query_weight, attn_out_weight, cotangent,
):
    pair = jnp.swapaxes(template_pair[0], 1, 2)
    row = lambda x: x.reshape(1, -1)
    every = functools.partial(lax.all_to_all, axis_name="row", split_axis=0, concat_axis=0, tiled=True)
    plane, half = (ROWS, C, N), (ROWS, 2 * C, N)
    sources = (
        left_weight, right_weight, row(norm_gain), relpos_table.T, row(residue_index), residue_index, template_mask,
        template_mask, pair, gate_weight, out_weight, kv_weight, row(tri_gain), row(pair_gain),
        query_pair, cotangent, row(query_gain), query_weight.T, attn_out_weight,
    )
    scratch = fetched(*sources)
    for n in (5, 7):
        scratch[1 + n] = pltpu.SMEM(sources[n].shape, sources[n].dtype)
    outs = [((SHARDS, 32, N), BF16), (plane, F32), ((ROWS, 1, N), F32), ((C, 8 * 128), BF16), ((3, C, 128), F32)]
    outs += [(plane, BF16)] + [(plane, F32)] * 3
    lr, z, pm, weights, gains, ln_b, qh, do, gate = call(
        project_kernel, outs, [HBM] * 19, [pltpu.VMEM((SHARDS, 32, ROWS * C), BF16)] + scratch
    )(*stay(*sources))
    tri, mats = call(tri_kernel, [((SHARDS, 16, N), BF16), ((4, N, N), BF16)], [VMEM])(every(lr))
    tri = every(tri)
    sg, that, yhat, upd, kv, rstd = call(
        attend_kernel,
        [((ROWS, 8, N), F32)] + [(plane, F32)] * 3 + [(half, BF16), ((ROWS, 8, N), F32)],
        [VMEM] * 8,
        [wide_scratch(SHARDS * 16)],
    )(tri, z, qh, do, gate, pm, weights, gains)
    sg = lax.all_gather(sg, "tmpl")
    dtri, dqh, d_y, d_gate = call(
        back_kernel,
        [((SHARDS, 16, N), BF16), (plane, F32), (plane, F32), (plane, BF16)],
        [VMEM] * 12,
        [wide_scratch(SHARDS * 16)],
    )(sg, that, yhat, gate, upd, qh, do, kv, rstd, pm, weights, gains)
    dlr, keep = call(tri_back_kernel, [((SHARDS, 32, N), BF16), ((HALF, C, N), BF16)], [VMEM] * 4)(
        every(dtri), mats, dqh, swap(dqh, 1)
    )
    dlr, keep = after(every(dlr), keep)
    proj, d = call(
        weight_kernel, [((C, 2 * C), F32), (half, BF16)], [VMEM] * 3, [wide_scratch(SHARDS * 32)]
    )(dlr, ln_b, pm)
    near = swap(proj, 1)
    (grad,) = call(pair_grad_kernel, [(plane, F32)], [VMEM] * 6)(d, z, d_y, d_gate, weights, gains)
    proj = proj + near
    (fan,) = call(fan_kernel, [((SHARDS, C, 2 * C), BF16)], [VMEM] * 2)(proj, swap(proj, 2))
    fan, grad, own = after(fan, grad, keep + swap(keep, 2))
    parts = every(fan)
    sources = (query_pair, row(query_gain), query_weight.T)
    (query_grad,) = call(
        query_grad_kernel, [((ROWS, N, 2 * C), F32)], [VMEM] * 2 + [HBM] * 3, fetched(*sources)
    )(own, swap(own, 1), *sources)
    parts, query_grad = after(parts, query_grad)
    (proj,) = call(sum_kernel, [((2, C, C), F32)], [VMEM])(parts)
    return jnp.swapaxes(grad, 1, 2)[None], query_grad, proj


def solution(mesh):
    in_specs = (
        P("tmpl", "row", None, None),
        P(),
        P(),
        P("row", None, None),
        *([P()] * 12),
        P("row", None, None),
    )
    out_specs = (P("tmpl", "row", None, None), P("row", None, None), P())
    return jax.shard_map(local, mesh=mesh, in_specs=in_specs, out_specs=out_specs, check_vma=False)
```

```python
import functools

import jax
import jax.numpy as jnp
from jax import lax
from jax.experimental import pallas as pl
from jax.experimental.pallas import tpu as pltpu
from jax.sharding import PartitionSpec as P

F32 = jnp.float32
BF16 = jnp.bfloat16
HEADS = 4
HEAD_DIM = 16
C = 64
ROWS = 8
N = 256
SHARDS = 32
UNROLL = 8
HALF = ROWS // 2
PIECES = 4
HBM = pl.BlockSpec(memory_space=pltpu.HBM)
VMEM = pl.BlockSpec(memory_space=pltpu.VMEM)


def dot(a, b, contract=((1,), (0,))):
    return lax.dot_general(a, b, (contract, ((), ())), preferred_element_type=F32)


def fine_dot(a, x, contract=((1,), (0,))):
    high = x.astype(BF16)
    low = (x - high.astype(F32)).astype(BF16)
    return dot(a, high, contract) + dot(a, low, contract)


def flip(x):
    return x.astype(F32).T


def column(row):
    return jnp.broadcast_to(row, (128, row.shape[1])).T


def twice(x):
    return jnp.concatenate([x, x], axis=1)


def slab(weights, n, width=C):
    return weights[:, 128 * n : 128 * n + width]


def hat(x):
    mean = jnp.mean(x, 0, keepdims=True)
    cent = x - mean
    var = jnp.mean(cent * cent, 0, keepdims=True)
    rstd = lax.rsqrt(var + 1e-05)
    return cent * rstd, rstd


def hat_back(dy, xhat, rstd):
    return rstd * (dy - jnp.mean(dy, 0, keepdims=True) - xhat * jnp.mean(dy * xhat, 0, keepdims=True))


def owner_rows(left, right):
    rows = jnp.concatenate([left, right], axis=0)
    rows = jnp.concatenate([rows, rows], axis=1)
    sub = lax.broadcasted_iota(jnp.int32, (8, 128), 0)
    lane = lax.broadcasted_iota(jnp.int32, (8, 128), 1) // C
    tiles = []
    for pair in range(ROWS // 2):
        mine = (sub == 2 * pair + lane)[None, None]
        spread = jnp.broadcast_to(rows.reshape(4, SHARDS, 1, 128), (4, SHARDS, 8, 128))
        tiles.append(jnp.where(mine, spread, 0.0))
    return tiles


def put_rows(spread, first, step, x):
    for half in range(2):
        spread[half, pl.ds(first, x.shape[0], stride=step), :] = x[:, 128 * half : 128 * half + 128]


def pack(spread, out):
    for half in range(2):
        rows = spread[half, : out.shape[0] * out.shape[1]]
        out[:, :, 128 * half : 128 * half + 128] = rows.reshape(out.shape[0], out.shape[1], 128).astype(BF16)


def take_rows(wide, first, step):
    return jnp.concatenate([wide[half, pl.ds(first, SHARDS, stride=step), :] for half in range(2)], axis=1)


def unpack(x, wide):
    rows = x.shape[0] * x.shape[1]
    for half in range(2):
        wide[half, :rows] = x[:, :, 128 * half : 128 * half + 128].astype(F32).reshape(rows, 128)


def place(rows_ref):
    t = lax.axis_index("tmpl")
    start = lax.axis_index("row") * ROWS
    mask_row = rows_ref[pl.ds(t, 1), :].astype(F32)
    return t, start, mask_row


def each_row(body, carry=0, rows=ROWS, unroll=UNROLL):
    def step(s, carry):
        for u in range(unroll):
            carry = body(s * unroll + u, carry)
        return carry

    if unroll == rows:
        return step(0, carry)
    return lax.fori_loop(0, rows // unroll, step, carry)


def copies(sources, places, sems, first=0):
    started = [pltpu.make_async_copy(src, dst, sems.at[first + n]) for n, (src, dst) in enumerate(zip(sources, places))]
    for copy in started:
        copy.start()
    return started


def arrive(started):
    for copy in started:
        copy.wait()


def relative(res_s, residues, table, at):
    bins = lax.broadcasted_iota(jnp.int32, (128, N), 0)
    offset = jnp.clip(res_s[at] - residues, -64, 63) + 64
    return dot(table, jnp.where(bins == offset, 1.0, 0.0).astype(BF16))


def project_kernel(*refs):
    sources, outs, places = refs[:19], refs[19:28], refs[30:]
    lhs, sems = refs[28:30]
    lr, z, pm, weights, gains, normed, qh_out, do_out, gate_out = outs
    arriving = copies(sources, places, sems)
    wl, wr, norm_gain, table_t, res, res_s, mask, mask_s, pair, wg, wo, wkv, tri_gain, pair_gain = places[:14]
    query, cot, q_gain, wq_t, wao = places[14:]
    arrive(arriving[:2])
    for pair_of, tile in enumerate(owner_rows(flip(wl[...]), flip(wr[...]))):
        for side in range(2):
            both = jnp.concatenate([tile[2 * side], tile[2 * side + 1]], axis=1)
            lhs[:, 16 * side : 16 * side + 16, 128 * pair_of : 128 * pair_of + 128] = both.astype(BF16)
    arrive(arriving[2:9])
    t, start, mask_row = place(mask)
    table, residues, gain = table_t[...], res[...], column(norm_gain[...])
    g = twice(gain)

    def body(i, carry):
        z_i = pair[i].astype(F32) + relative(res_s, residues, table, start + i)
        z[i] = z_i
        pm_i = mask_row * mask_s[t, start + i].astype(F32)
        pm[i] = pm_i
        normed[i] = (hat(z_i)[0] * g).astype(BF16)
        return carry

    each_row(body)
    arrive(arriving[9:])
    blank = jnp.zeros((C, C), BF16)
    wkv_t = flip(wkv[...]).astype(BF16)
    parts = [wkv[...], wl[...], wr[...], flip(wo[...]).astype(BF16), blank, wo[...], blank, wg[...], blank]
    parts += [wkv_t[:C], blank, wkv_t[C:], blank, flip(wg[...]).astype(BF16), blank]
    weights[...] = jnp.concatenate(parts, axis=1)
    gains[0] = gain
    gains[1] = column(tri_gain[...])
    gains[2] = column(pair_gain[...])
    some = SHARDS // PIECES
    for p in range(PIECES):
        owners = slice(p * some, (p + 1) * some)
        both = dot(lhs[owners].reshape(some * 32, ROWS * C), normed[...].reshape(ROWS * C, N)).reshape(some * 4, ROWS, N)
        lr[owners] = (both * pm[...].reshape(1, ROWS, N)).reshape(some, 32, N).astype(BF16)

    wg_t = flip(wg[...]).astype(BF16)
    wq_v, wao_v, g_query = wq_t[...], wao[...], q_gain[...]

    def heads(i, carry):
        x = query[i].astype(F32)
        cent = x - jnp.mean(x, -1, keepdims=True)
        var = jnp.mean(cent * cent, -1, keepdims=True)
        qn = cent * lax.rsqrt(var + 1e-05) * g_query
        qh_out[i] = fine_dot(wq_v, qn, ((1,), (1,))) * HEAD_DIM ** (-0.5)
        do_out[i] = dot(wao_v, cot[i], ((1,), (1,)))
        gate_out[i] = jax.nn.sigmoid(fine_dot(wg_t, hat(z[i])[0] * g))
        return carry

    each_row(heads)


def tri_kernel(lr, tri_out, mats_out):
    wide = lr[...].astype(F32)
    mats = [wide[:, 8 * q : 8 * q + 8, :].reshape(N, N).astype(BF16) for q in range(4)]
    for q in range(4):
        mats_out[q] = mats[q]
    parts = [dot(mats[cc], mats[2 + cc], ((1,), (1,))).reshape(SHARDS, 8, N) for cc in range(2)]
    tri_out[...] = jnp.concatenate(parts, axis=1).astype(BF16)


def heads_sum(x):
    return jnp.sum(x.reshape(HEADS, HEAD_DIM, N), axis=1)


def heads_spread(x):
    return jnp.broadcast_to(x[:, None, :], (HEADS, HEAD_DIM, N)).reshape(C, N)


def attend_kernel(
    tri, z, qh, do, gate, pm, weights, gains, sg_out, that_out, yhat_out, upd_out, kv_out, rstd_out, wide
):
    unpack(tri, wide)
    wo_t = slab(weights, 2)
    wkv_t = jnp.concatenate([slab(weights, 5), slab(weights, 6)], axis=0)
    g_tri, g_pair = twice(gains[1]), twice(gains[2])

    def body(i, carry):
        tri_i = jnp.concatenate([take_rows(wide, i, 16), take_rows(wide, 8 + i, 16)], axis=0)
        that, rstd_t = hat(tri_i)
        upd = fine_dot(wo_t, that * g_tri)
        yhat, rstd_y = hat(z[i] + gate[i] * upd)
        kv = fine_dot(wkv_t, yhat * g_pair).astype(BF16)
        kv_f = kv.astype(F32)
        score = heads_sum(qh[i] * kv_f[:C]) * pm[i] + (pm[i] - 1.0) * 1000000000.0
        dot_v = heads_sum(do[i] * kv_f[C:])
        sg_out[i] = jnp.concatenate([score, dot_v], axis=0)
        that_out[i] = that
        yhat_out[i] = yhat
        upd_out[i] = upd
        kv_out[i] = kv
        rstd_out[i] = jnp.concatenate([jnp.broadcast_to(rstd_t, (4, N)), jnp.broadcast_to(rstd_y, (4, N))], axis=0)
        return carry

    each_row(body)


def back_kernel(
    sg, that, yhat, gate, upd, qh, do, kv, rstd, pm, weights, gains,
    dtri_out, dqh_out, dy_out, dgate_out, spread,
):
    t = lax.axis_index("tmpl")
    core = t % 2
    g_tri, g_pair = twice(gains[1]), twice(gains[2])
    wkv_v, wo_v = slab(weights, 0, 2 * C), slab(weights, 3)

    def row(i, n):
        every = [sg[s, i] for s in range(4)]
        own = sg[t, i]
        top = jnp.maximum(jnp.maximum(every[0][:4], every[1][:4]), jnp.maximum(every[2][:4], every[3][:4]))
        expo = [jnp.exp(e[:4] - top) for e in every]
        inv = 1.0 / (expo[0] + expo[1] + expo[2] + expo[3])
        delta = sum(ex * e[4:] for ex, e in zip(expo, every)) * inv
        prob = jnp.exp(own[:4] - top) * inv
        ds = heads_spread(pm[i] * prob * (own[4:] - delta))
        dqh_out[n] = ds * kv[i].astype(F32)[:C]
        d_kv = jnp.concatenate([ds * qh[i], heads_spread(prob) * do[i]], axis=0).astype(BF16)
        rs = rstd[i]
        d_y = hat_back(dot(wkv_v, d_kv) * g_pair, yhat[i], rs[4:5])
        gate_i = gate[i]
        d_upd = d_y * gate_i
        d_gate = (d_upd * upd[i] * (1.0 - gate_i)).astype(BF16)
        dy_out[i] = d_y
        dgate_out[i] = d_gate
        d_tri = hat_back(dot(wo_v, d_upd.astype(BF16)) * g_tri, that[i], rs[0:1])
        put_rows(spread, i, 16, d_tri[:32])
        put_rows(spread, 8 + i, 16, d_tri[32:])

    def body(n, carry):
        row(core * HALF + n, n)
        row((1 - core) * HALF + n, HALF + n)
        return carry

    each_row(body, rows=HALF, unroll=UNROLL // 2)
    pack(spread, dtri_out)


def tri_back_kernel(dtri, mats, dqh, near, out, keep_out):
    keep_out[...] = (dqh[:HALF] + near[HALF:]).astype(BF16)
    wide = dtri[...].astype(F32)
    d = [wide[:, 8 * cc : 8 * cc + 8, :].reshape(N, N).astype(BF16) for cc in range(2)]
    parts = [dot(d[cc], mats[2 + cc]) for cc in range(2)]
    parts += [dot(d[cc], mats[cc], ((0,), (0,))) for cc in range(2)]
    out[...] = jnp.concatenate([p.reshape(SHARDS, 8, N) for p in parts], axis=1).astype(BF16)


def weight_kernel(dlr, ln_b, pm, proj_out, d_out, wide):
    unpack(dlr, wide)

    def body(i, total):
        parts = [take_rows(wide, 8 * q + i, 32) for q in range(4)]
        d = (jnp.concatenate(parts, axis=0) * pm[i]).astype(BF16)
        d_out[i] = d
        return total + dot(ln_b[i], d, ((1,), (1,)))

    proj_out[...] = each_row(body, jnp.zeros((C, 2 * C), F32))


def pair_grad_kernel(d, z, d_y, d_gate, weights, gains, grad_out):
    g = twice(gains[0])
    weight = jnp.concatenate([slab(weights, 1, 2 * C), slab(weights, 4)], axis=1)

    def body(i, carry):
        zhat, rstd = hat(z[i])
        d_ln = dot(weight, jnp.concatenate([d[i], d_gate[i]], axis=0))
        grad_out[i] = d_y[i] + hat_back(d_ln * g, zhat, rstd)
        return carry

    each_row(body)


def query_grad_kernel(own, other, query_h, gain_h, wq_h, out, sems, query, gain, wq_t):
    arrive(copies((query_h, gain_h, wq_h), (query, gain, wq_t), sems))
    core = lax.axis_index("tmpl") % 2
    g = gain[...] * HEAD_DIM ** (-0.5)
    wq_v = wq_t[...]

    def body(i, d_qh):
        x = query[i].astype(F32)
        cent = x - jnp.mean(x, -1, keepdims=True)
        var = jnp.mean(cent * cent, -1, keepdims=True)
        rstd = lax.rsqrt(var + 1e-05)
        xhat = cent * rstd
        dy = dot(d_qh, wq_v, ((0,), (0,))) * g
        out[i] = rstd * (dy - jnp.mean(dy, -1, keepdims=True) - xhat * jnp.mean(dy * xhat, -1, keepdims=True))

    for i in range(HALF):
        body(core * HALF + i, own[i])
        body((1 - core) * HALF + i, other[i])


def fan_kernel(own, far, out, some, sems):
    total = (own[...] + far[...]).astype(BF16)
    for s in range(some.shape[0]):
        some[s] = total
    spots = [out.at[pl.ds(at, some.shape[0])] for at in range(0, SHARDS, some.shape[0])]
    arrive(copies([some] * len(spots), spots, sems))


def sum_kernel(parts, out):
    total = jnp.sum(parts[...].astype(F32), axis=0)
    out[0] = total[:, :C]
    out[1] = total[:, C:]


def call(kernel, outs, specs, scratch=(), vmem=40, home=VMEM):
    return pl.pallas_call(
        kernel,
        out_shape=[jax.ShapeDtypeStruct(s, d) for s, d in outs],
        in_specs=specs,
        out_specs=[home] * len(outs),
        scratch_shapes=list(scratch),
        compiler_params=pltpu.CompilerParams(vmem_limit_bytes=vmem * 1024 * 1024),
    )


def wide_scratch(rows):
    return pltpu.VMEM((2, rows + rows // SHARDS, 128), F32)


def fetched(*arrays):
    return [pltpu.SemaphoreType.DMA((len(arrays),))] + [pltpu.VMEM(a.shape, a.dtype) for a in arrays]


def stay(*arrays):
    return [pltpu.with_memory_space_constraint(a, pltpu.HBM) for a in arrays]


def swap(x, bit):
    return lax.ppermute(x, "tmpl", [(i, i ^ bit) for i in range(4)])


def after(x, *others):
    return lax.optimization_barrier((x, *others))


def local(
    template_pair, template_mask, residue_index, query_pair, relpos_table, norm_gain, left_weight, right_weight,
    gate_weight, out_weight, tri_gain, pair_gain, kv_weight, query_gain, query_weight, attn_out_weight, cotangent,
):
    pair = jnp.swapaxes(template_pair[0], 1, 2)
    row = lambda x: x.reshape(1, -1)
    every = functools.partial(lax.all_to_all, axis_name="row", split_axis=0, concat_axis=0, tiled=True)
    plane, half = (ROWS, C, N), (ROWS, 2 * C, N)
    sources = (
        left_weight, right_weight, row(norm_gain), relpos_table.T, row(residue_index), residue_index, template_mask,
        template_mask, pair, gate_weight, out_weight, kv_weight, row(tri_gain), row(pair_gain),
        query_pair, cotangent, row(query_gain), query_weight.T, attn_out_weight,
    )
    scratch = fetched(*sources)
    for n in (5, 7):
        scratch[1 + n] = pltpu.SMEM(sources[n].shape, sources[n].dtype)
    outs = [((SHARDS, 32, N), BF16), (plane, F32), ((ROWS, 1, N), F32), ((C, 8 * 128), BF16), ((3, C, 128), F32)]
    outs += [(plane, BF16)] + [(plane, F32)] * 3
    lr, z, pm, weights, gains, ln_b, qh, do, gate = call(
        project_kernel, outs, [HBM] * 19, [pltpu.VMEM((SHARDS, 32, ROWS * C), BF16)] + scratch
    )(*stay(*sources))
    tri, mats = call(tri_kernel, [((SHARDS, 16, N), BF16), ((4, N, N), BF16)], [VMEM])(every(lr))
    tri = every(tri)
    sg, that, yhat, upd, kv, rstd = call(
        attend_kernel,
        [((ROWS, 8, N), F32)] + [(plane, F32)] * 3 + [(half, BF16), ((ROWS, 8, N), F32)],
        [VMEM] * 8,
        [wide_scratch(SHARDS * 16)],
    )(tri, z, qh, do, gate, pm, weights, gains)
    sg = lax.all_gather(sg, "tmpl")
    dtri, dqh, d_y, d_gate = call(
        back_kernel,
        [((SHARDS, 16, N), BF16), (plane, F32), (plane, F32), (plane, BF16)],
        [VMEM] * 12,
        [wide_scratch(SHARDS * 16)],
    )(sg, that, yhat, gate, upd, qh, do, kv, rstd, pm, weights, gains)
    dlr, keep = call(tri_back_kernel, [((SHARDS, 32, N), BF16), ((HALF, C, N), BF16)], [VMEM] * 4)(
        every(dtri), mats, dqh, swap(dqh, 1)
    )
    dlr, keep = after(every(dlr), keep)
    proj, d = call(
        weight_kernel, [((C, 2 * C), F32), (half, BF16)], [VMEM] * 3, [wide_scratch(SHARDS * 32)]
    )(dlr, ln_b, pm)
    near = swap(proj, 1)
    (grad,) = call(pair_grad_kernel, [(plane, F32)], [VMEM] * 6)(d, z, d_y, d_gate, weights, gains)
    proj = proj + near
    (fan,) = call(
        fan_kernel,
        [((SHARDS, C, 2 * C), BF16)],
        [VMEM] * 2,
        [pltpu.VMEM((8, C, 2 * C), BF16), pltpu.SemaphoreType.DMA((SHARDS // 8,))],
        home=HBM,
    )(proj, swap(proj, 2))
    fan, grad, own = after(fan, grad, keep + swap(keep, 2))
    parts = every(fan)
    sources = (query_pair, row(query_gain), query_weight.T)
    (query_grad,) = call(
        query_grad_kernel, [((ROWS, N, 2 * C), F32)], [VMEM] * 2 + [HBM] * 3, fetched(*sources)
    )(own, swap(own, 1), *sources)
    parts, query_grad = after(parts, query_grad)
    (proj,) = call(sum_kernel, [((2, C, C), F32)], [VMEM])(parts)
    return jnp.swapaxes(grad, 1, 2)[None], query_grad, proj


def solution(mesh):
    in_specs = (
        P("tmpl", "row", None, None),
        P(),
        P(),
        P("row", None, None),
        *([P()] * 12),
        P("row", None, None),
    )
    out_specs = (P("tmpl", "row", None, None), P("row", None, None), P())
    return jax.shard_map(local, mesh=mesh, in_specs=in_specs, out_specs=out_specs, check_vma=False)
```
